256 devices in a mesh: tm: 128 (over x, z, y_hi, core), mp: 2 (over y_lo).
Axes of the slice: x: 4, y: 4 (y_hi: 2, y_lo: 2; y = y_hi * 2 + y_lo), z: 8, core: 2. Of those that a mesh axis runs over, the one named last changes fastest.
Arguments:
- patches: bfloat16 [20480, 768], P('tm'), may hold values from -6 to 6
- keep_mask: int32 [20480], replicated, may hold values from 0 to 1, as said below
- segment: int32 [20480], replicated, may hold values from 0 to 255, never falling along the last dimension, each value on 1 to 160 neighbouring positions
- w_query: bfloat16 [768, 768], P(None, 'mp'), may hold values from -0.4375 to 0.4375
- w_key: bfloat16 [768, 768], P(None, 'mp'), may hold values from -0.4375 to 0.4375
- w_value: bfloat16 [768, 768], P(None, 'mp'), may hold values from -0.21875 to 0.21875
- w_out: bfloat16 [768, 768], P('mp'), may hold values from -0.4375 to 0.4375
- w_cross_query: bfloat16 [768, 768], P(None, 'mp'), may hold values from -0.375 to 0.375
- w_cross_out: bfloat16 [768, 768], P('mp'), may hold values from -0.21875 to 0.21875
- w_up: bfloat16 [768, 3072], P(None, 'mp'), may hold values from -0.21875 to 0.21875
- w_down: bfloat16 [3072, 768], P('mp'), may hold values from -0.109375 to 0.109375
Outputs:
- updated: bfloat16 [20480, 768], P('tm')
The draws below stay inside these ranges and needn't reach their ends.
Inputs may be any that keep to these rules, and one draw needn't show every extreme that they name: `keep_mask`: each run of 160 patches from the start (one index of tm) keeps between 24 and 72 patches, 6144 in all; the kept patches before the j-th run number j * 48 plus at most 12 and minus at most 12, with a difference of exactly 12 in some run; some run keeps exactly 72. Segment numbers never fall along the patches; each segment covers 1 to 160 patches, one exactly 160.
All inputs are finite; a program needn't handle non-finite values.
Results may differ from the reference program's by a relative error of at most 0.0081.
Values may be sent and summed in bfloat16 or wider, within the bound.
A program may use at most 128 MiB of HBM per device.

```python
import math
import jax
import jax.numpy as jnp
import numpy as np
from jax import lax

D = 768
HEADS = 12
HD = 64
FF = 3072
P_DEV = 160
KEPT_DEV = 48
DRIFT = 12
TOKENS = 20480
TOTAL_KEPT = 6144
SEGMENTS = 256
N_TM = 128


def draw_keep_mask(key, part):
    device_count = TOKENS // P_DEV
    key_drift, key_place, key_order = jax.random.split(jax.random.fold_in(key, 11), 3)
    drift = jax.random.randint(key_drift, (device_count + 1,), -DRIFT, DRIFT + 1, dtype=jnp.int32)
    chosen = jax.random.randint(key_place, (), 1, device_count - 1, dtype=jnp.int32)
    index = jnp.arange(device_count + 1, dtype=jnp.int32)
    drift = jnp.where(index == chosen, -DRIFT, drift)
    drift = jnp.where(index == chosen + 1, DRIFT, drift)
    drift = jnp.where((index == 0) | (index == device_count), 0, drift)
    counts = KEPT_DEV + drift[1:] - drift[:-1]
    order_keys = jax.random.split(key_order, device_count)
    orders = jax.vmap(lambda single: jax.random.permutation(single, jnp.arange(P_DEV, dtype=jnp.int32)))(order_keys)
    return (orders < counts[:, None]).astype(jnp.int32).reshape(-1)


def steps_of(own_key, dims, shards, smallest, high):
    loudness, own = 1.0, jax.random.fold_in(own_key, 6)
    for dim, blocks in shards:
        draws = jnp.exp(jax.random.uniform(jax.random.fold_in(own, dim), (blocks,), jnp.float32, smallest / len(shards), high / len(shards)))
        loudness = loudness * jnp.repeat(draws, dims[dim] // blocks).reshape([-1 if axis == dim else 1 for axis in range(len(dims))])
    return loudness


def length_profile(count, total, bound, skew):
    portions = [(1 << 20) // math.isqrt(rank ** skew) + 1 for rank in range(2, count + 1)]
    rest, given = total - bound - (count - 1), [1] * (count - 1)
    while rest > 0:
        free = [i for i in range(count - 1) if given[i] < bound]
        mass, remaining = sum([portions[i] for i in free]), rest
        for i in free:
            extra = min(bound - given[i], max(1, remaining * portions[i] // mass), rest)
            given[i] = given[i] + extra
            rest = rest - extra
    return np.array([bound] + given)


def uneven_parts(stream_key, count, total, most, slope):
    if count == 2:
        one = jax.random.randint(stream_key, (), max(1, total - most), min(most, total - 1) + 1)
        return jnp.stack([one, total - one])
    sizes = jnp.asarray(length_profile(count, total, most, slope), jnp.int32)
    pairs = (count - 1) // 2
    giver, sink = sizes[1:1 + 2 * pairs:2], sizes[2:2 + 2 * pairs:2]
    room = jnp.minimum(giver - 1, most - sink)
    passed = jax.random.randint(jax.random.fold_in(stream_key, 1), (pairs,), 0, 1 << 20) % (room + 1)
    sizes = sizes.at[1:1 + 2 * pairs:2].set(giver - passed).at[2:2 + 2 * pairs:2].set(sink + passed)
    return sizes[jax.random.permutation(jax.random.fold_in(stream_key, 2), count)]


def centred(rng, extent, scale, bound, cuts=(), held_as=jnp.bfloat16):
    values = scale * jax.random.normal(rng, extent, jnp.float32)
    if cuts:
        values = values * steps_of(rng, extent, cuts, -0.22, 0.18)
    return jnp.clip(values, -bound, bound).astype(held_as)


def setup_inputs(seed: int = 0) -> dict:
    arg_keys = jax.random.split(jax.random.key(seed), 12)
    return {
        "patches": centred(arg_keys[0], (TOKENS, D), 1.0, 6.0, ((0, 128),)),
        "keep_mask": draw_keep_mask(jax.random.fold_in(arg_keys[11], 71), 0),
        "segment": jnp.searchsorted(jnp.cumsum(uneven_parts(arg_keys[2], SEGMENTS, TOKENS, P_DEV, 1)), jnp.arange(TOKENS), side="right").astype(jnp.int32),
        "w_query": centred(arg_keys[3], (D, D), (D // 4) ** -0.5, 0.4375, ((1, 2),)),
        "w_key": centred(arg_keys[4], (D, D), (D // 4) ** -0.5, 0.4375, ((1, 2),)),
        "w_value": centred(arg_keys[5], (D, D), D ** -0.5, 0.21875, ((1, 2),)),
        "w_out": centred(arg_keys[6], (D, D), (D // 4) ** -0.5, 0.4375, ((0, 2),)),
        "w_cross_query": centred(arg_keys[7], (D, D), (D // 3) ** -0.5, 0.375, ((1, 2),)),
        "w_cross_out": centred(arg_keys[8], (D, D), D ** -0.5, 0.21875, ((0, 2),)),
        "w_up": centred(arg_keys[9], (D, FF), D ** -0.5, 0.21875, ((1, 2),)),
        "w_down": centred(arg_keys[10], (FF, D), FF ** -0.5, 0.109375, ((0, 2),)),
    }


def norm_rows(values):
    values = values.astype(jnp.float32)
    center = values - lax.optimization_barrier(jnp.mean(values, axis=-1, keepdims=True))
    return center * lax.rsqrt(lax.optimization_barrier(jnp.mean(center * center, axis=-1, keepdims=True)) + 1e-05)

def split_heads(values):
    return values.reshape(values.shape[0], HEADS, HD)

def attend(queries, key_heads, value_heads, usable):
    query_heads = split_heads(queries).astype(jnp.float32)
    scores = jnp.einsum('rhe,mhe->rhm', query_heads, key_heads) * HD ** (-0.5)
    weight = jnp.where(usable[:, None, :], jnp.exp(scores), jnp.float32(0.0))
    rounded = lax.optimization_barrier(weight.astype(jnp.bfloat16)).astype(jnp.float32)
    numerator = jnp.einsum('rhm,mhe->rhe', rounded, value_heads)
    result = numerator / lax.optimization_barrier(jnp.sum(weight, axis=-1))[:, :, None]
    return result.astype(jnp.bfloat16).reshape(queries.shape[0], D)

def reference(patches, keep_mask, segment, w_query, w_key, w_value, w_out, w_cross_query, w_cross_out, w_up, w_down):
    normed = norm_rows(patches).astype(jnp.bfloat16)
    key_all = jnp.dot(normed, w_key, preferred_element_type=jnp.float32).astype(jnp.bfloat16)
    value_all = jnp.dot(normed, w_value, preferred_element_type=jnp.float32).astype(jnp.bfloat16)
    cross_query = jnp.dot(normed, w_cross_query, preferred_element_type=jnp.float32).astype(jnp.bfloat16)
    positions = jnp.nonzero(keep_mask, size=TOTAL_KEPT)[0].astype(jnp.int32)
    kept_patches = patches[positions]
    kept_query = jnp.dot(normed[positions], w_query, preferred_element_type=jnp.float32).astype(jnp.bfloat16)
    kept_keys = split_heads(key_all[positions]).astype(jnp.float32)
    kept_values = split_heads(value_all[positions]).astype(jnp.float32)
    every_pair = jnp.ones((1, TOTAL_KEPT), dtype=bool)

    def kept_block(queries):
        return attend(queries, kept_keys, kept_values, every_pair)
    kept_attention = lax.map(kept_block, kept_query.reshape(N_TM, KEPT_DEV, D)).reshape(TOTAL_KEPT, D)
    hidden = kept_patches.astype(jnp.float32) + jnp.dot(kept_attention, w_out, preferred_element_type=jnp.float32)
    normed_hidden = norm_rows(hidden).astype(jnp.bfloat16)
    gated = jax.nn.gelu(jnp.dot(normed_hidden, w_up, preferred_element_type=jnp.float32), approximate=True).astype(jnp.bfloat16)
    kept_result = (hidden + jnp.dot(gated, w_down, preferred_element_type=jnp.float32)).astype(jnp.bfloat16)
    zero_rows = jnp.zeros((P_DEV, D), jnp.bfloat16)
    padded_keys = jnp.concatenate([zero_rows, key_all, zero_rows], axis=0)
    padded_values = jnp.concatenate([zero_rows, value_all, zero_rows], axis=0)
    padded_mask = jnp.concatenate([jnp.zeros((P_DEV,), jnp.int32), keep_mask, jnp.zeros((P_DEV,), jnp.int32)])
    padded_segment = jnp.concatenate([jnp.full((P_DEV,), -1, jnp.int32), segment, jnp.full((P_DEV,), -1, jnp.int32)])
    query_index = jnp.arange(P_DEV, dtype=jnp.int32)
    key_index = jnp.arange(3 * P_DEV, dtype=jnp.int32)

    def cross_block(block_index):
        start = (block_index * P_DEV).astype(jnp.int32)
        queries = lax.dynamic_slice_in_dim(cross_query, start, P_DEV, 0)
        own_segment = lax.dynamic_slice_in_dim(segment, start, P_DEV, 0)
        near_keys = lax.dynamic_slice_in_dim(padded_keys, start, 3 * P_DEV, 0)
        near_values = lax.dynamic_slice_in_dim(padded_values, start, 3 * P_DEV, 0)
        near_mask = lax.dynamic_slice_in_dim(padded_mask, start, 3 * P_DEV, 0)
        near_segment = lax.dynamic_slice_in_dim(padded_segment, start, 3 * P_DEV, 0)
        usable = (near_mask[None, :] == 1) & (near_segment[None, :] == own_segment[:, None]) | (key_index[None, :] == query_index[:, None] + P_DEV)
        return attend(queries, split_heads(near_keys).astype(jnp.float32), split_heads(near_values).astype(jnp.float32), usable)
    cross_attention = lax.map(cross_block, jnp.arange(N_TM, dtype=jnp.int32)).reshape(TOKENS, D)
    pruned_result = (patches.astype(jnp.float32) + jnp.dot(cross_attention, w_cross_out, preferred_element_type=jnp.float32)).astype(jnp.bfloat16)
    return pruned_result.at[positions].set(kept_result)
```

```python
import functools

import jax
import jax.numpy as jnp
from jax import lax
from jax.experimental import pallas as pl
from jax.experimental.pallas import tpu as pltpu
from jax.sharding import PartitionSpec as P

KEPT = 48
EDGE = 16
WINDOW = KEPT + 2 * EDGE
F32 = jnp.float32
BF16 = jnp.bfloat16


def norm_rows(values):
    values = values.astype(F32)
    center = values - jnp.mean(values, axis=-1, keepdims=True)
    return center * lax.rsqrt(jnp.mean(center * center, axis=-1, keepdims=True) + 1e-05)


def dot(a, b):
    return jnp.dot(a, b, preferred_element_type=F32)


def dot_t(a, b):
    return lax.dot_general(a, b, (((1,), (1,)), ((), ())), preferred_element_type=F32)


def dot_0(a, b):
    return lax.dot_general(a, b, (((0,), (0,)), ((), ())), preferred_element_type=F32)


def iota(shape, dim):
    return lax.broadcasted_iota(jnp.int32, shape, dim)


def attend_pair(queries, keys, values, usable):
    rows = queries.shape[0]
    low = iota((rows, 128), 1) < 64
    zero = jnp.zeros_like(queries)
    both = jnp.concatenate([jnp.where(low, queries, zero), jnp.where(low, zero, queries)], axis=0)
    weight = jnp.exp(dot_t(both, keys))
    if usable is not None:
        weight = jnp.where(usable, weight, 0.0)
    ones = jnp.ones((keys.shape[0], 128), BF16)
    total = dot(weight.astype(BF16), jnp.concatenate([values, ones], axis=1))
    numerator = jnp.where(low, total[:rows, :128], total[rows:, :128])
    denominator = jnp.where(low, total[:rows, 128:], total[rows:, 128:])
    return numerator, denominator


def kernel(
    nx,
    nz,
    patches_ref,
    mask_ref,
    seg_ref,
    wq_hbm,
    wk_hbm,
    wv_hbm,
    wo_hbm,
    wcq_hbm,
    wco_hbm,
    wu_hbm,
    wd_hbm,
    out_ref,
    wproj,
    wo,
    wco,
    wu,
    wd,
    xwin,
    lwin,
    rwin,
    kvbuf,
    qbuf,
    rsout,
    rsin,
    keys,
    attn_out,
    attn_in,
    cross_out,
    cross_in,
    down_out,
    down_in,
    result,
    left_result,
    right_result,
    wsem,
    ssem,
    rsem,
):
    ntm = nx * nz * 4
    rows_dev, width = patches_ref.shape
    half = wq_hbm.shape[1]
    me = lax.axis_index("tm")
    mp = lax.axis_index("mp")
    core = lax.rem(me, 2)
    yh = lax.rem(me // 2, 2)
    z = lax.rem(me // 4, nz)
    x = me // (4 * nz)
    sibling = me + 1 - 2 * core
    ypart = me + 2 - 4 * yh
    right = lax.rem(me + 1, ntm)
    left = lax.rem(me + ntm - 1, ntm)
    zpeer = [me + 4 * (lax.rem(z + k, nz) - z) for k in range(nz)]
    xpeer = [me + 4 * nz * (lax.rem(x + k, nx) - x) for k in range(nx)]

    weights = [
        (wq_hbm, wproj.at[:, 0:half]),
        (wk_hbm, wproj.at[:, half : 2 * half]),
        (wv_hbm, wproj.at[:, 2 * half : 3 * half]),
        (wcq_hbm, wproj.at[:, 3 * half : 4 * half]),
        (wco_hbm, wco),
        (wo_hbm, wo),
        (wu_hbm, wu),
        (wd_hbm, wd),
    ]
    loads = []
    for i, (source, target) in enumerate(weights):
        load = pltpu.make_async_copy(source, target, wsem.at[i])
        load.start()
        loads.append(load)

    barrier = pltpu.get_barrier_semaphore()
    greeted = [(sibling, mp), (ypart, mp), (right, mp), (left, mp), (me, 1 - mp)]
    greeted += [(peer, mp) for peer in zpeer[1:]] + [(peer, mp) for peer in xpeer[1:]]
    for target in greeted:
        pl.semaphore_signal(
            barrier, inc=1, device_id=target, device_id_type=pl.DeviceIdType.MESH
        )

    counter = [0]
    started = []

    def send(source, target, where):
        i = counter[0]
        counter[0] += 1
        copy = pltpu.make_async_remote_copy(
            src_ref=source,
            dst_ref=target,
            send_sem=ssem.at[i],
            recv_sem=rsem.at[i],
            device_id=where,
            device_id_type=pl.DeviceIdType.MESH,
        )
        copy.start()
        started.append(copy)
        return copy

    mask = mask_ref[...].astype(F32)
    before = jnp.where(iota(mask.shape, 0) < me, mask, 0.0)
    base = jnp.sum(jnp.sum(before, axis=1, keepdims=True), axis=0, keepdims=True)
    base = base - (KEPT * me).astype(F32)
    own_mask = mask_ref[pl.ds(me, 1), :].astype(F32)
    left_mask = jnp.where(me > 0, mask_ref[pl.ds(left, 1), :].astype(F32), 0.0)
    right_mask = jnp.where(me < ntm - 1, mask_ref[pl.ds(right, 1), :].astype(F32), 0.0)
    own_seg = seg_ref[pl.ds(me, 1), :].astype(F32) + 1.0
    left_seg = seg_ref[pl.ds(left, 1), :].astype(F32) + 1.0
    right_seg = seg_ref[pl.ds(right, 1), :].astype(F32) + 1.0
    earlier = (iota((rows_dev, rows_dev), 0) < iota((rows_dev, rows_dev), 1)).astype(F32)
    earlier = earlier.astype(BF16)

    def window(mask_row, base_row):
        rank = dot(jnp.broadcast_to(mask_row, (16, rows_dev)).astype(BF16), earlier)[0:1]
        slot = jnp.where(mask_row > 0.5, rank + base_row + float(EDGE), -1.0)
        grid = iota((WINDOW, rows_dev), 0).astype(F32)
        return jnp.where(grid == slot, 1.0, 0.0).astype(BF16)

    own_place = window(own_mask, base)
    patches = patches_ref[...]
    xwin[...] = dot(own_place, patches).astype(BF16)

    pl.semaphore_wait(barrier, len(greeted))

    edge_right = send(
        xwin.at[WINDOW - EDGE : WINDOW], lwin.at[WINDOW - EDGE : WINDOW], (right, mp)
    )
    edge_left = send(xwin.at[0:EDGE], rwin.at[0:EDGE], (left, mp))

    own_count = jnp.sum(own_mask, axis=1, keepdims=True)
    left_count = jnp.sum(left_mask, axis=1, keepdims=True)
    left_place = window(left_mask, base - left_count + float(KEPT))
    right_place = window(right_mask, base + own_count - float(KEPT))

    def key_segments(mask_place, seg_row):
        return dot_t(jnp.broadcast_to(seg_row, (16, rows_dev)).astype(BF16), mask_place)[0:1]

    key_seg = jnp.concatenate(
        [
            jnp.where(own_mask > 0.5, own_seg, 0.0),
            key_segments(left_place, left_seg),
            key_segments(right_place, right_seg),
        ],
        axis=1,
    )
    nkeys = rows_dev + 2 * WINDOW
    same = iota((rows_dev, rows_dev), 0) == iota((rows_dev, rows_dev), 1)
    seg_diag = jnp.where(same, own_seg, 0.0).astype(BF16)
    mask_diag = jnp.where(same, own_mask, 0.0).astype(BF16)
    query_seg = dot(seg_diag, jnp.ones((rows_dev, nkeys), BF16))
    usable = (query_seg == key_seg) | (
        iota((rows_dev, nkeys), 0) == iota((rows_dev, nkeys), 1)
    )
    usable = jnp.where(usable, 1.0, 0.0)
    usable = jnp.concatenate([usable, usable], axis=0) > 0.5
    kept_column = dot(mask_diag, jnp.ones((rows_dev, width), BF16)) > 0.5
    normed = norm_rows(patches).astype(BF16)

    edge_right.wait_recv()
    edge_left.wait_recv()
    own_rows = xwin[EDGE : EDGE + KEPT].astype(F32)
    kept = jnp.concatenate(
        [
            own_rows[:EDGE]
            + jnp.where(me > 0, lwin[WINDOW - EDGE : WINDOW].astype(F32), 0.0),
            own_rows[EDGE : KEPT - EDGE],
            own_rows[KEPT - EDGE :] + jnp.where(me < ntm - 1, rwin[0:EDGE].astype(F32), 0.0),
        ],
        axis=0,
    )
    for load in loads[:3]:
        load.wait()
    qkv = dot(norm_rows(kept).astype(BF16), wproj[:, : 3 * half])
    qbuf[0:KEPT] = (qkv[:, :half].astype(BF16).astype(F32) * 0.125).astype(BF16)
    kvbuf[0:KEPT] = qkv[:, half:].astype(BF16)

    def slots(ref, first, count):
        return ref.at[first * KEPT : (first + count) * KEPT]

    kv_y = send(slots(kvbuf, 0, 1), slots(kvbuf, nx, 1), (ypart, mp))
    kv_x = [
        send(slots(kvbuf, 0, 1), slots(kvbuf, nx - k, 1), (xpeer[k], mp)) for k in range(1, nx)
    ]
    far_first = sorted(range(1, nz), key=lambda k: -min(k, nz - k))
    q_z = [send(slots(qbuf, 0, 1), slots(qbuf, nz - k, 1), (zpeer[k], mp)) for k in far_first]
    kv_s = [send(slots(kvbuf, 0, 1), slots(kvbuf, 2 * nx, 1), (sibling, mp))]
    halo_right = send(xwin.at[0 : WINDOW - EDGE], lwin.at[0 : WINDOW - EDGE], (right, mp))
    halo_left = send(xwin.at[EDGE:WINDOW], rwin.at[EDGE:WINDOW], (left, mp))

    loads[3].wait()
    own_proj = dot(normed, wproj[:, half:])
    keys[0:rows_dev] = own_proj[:, : 2 * half].astype(BF16)
    cross_query = (own_proj[:, 2 * half :].astype(BF16).astype(F32) * 0.125).astype(BF16)

    kv_y.wait_recv()
    kv_x2 = [
        send(slots(kvbuf, nx, 1), slots(kvbuf, 2 * nx - k, 1), (xpeer[k], mp))
        for k in range(1, nx)
    ]

    halo_right.wait_recv()
    halo_left.wait_recv()
    near = jnp.concatenate([lwin[...], rwin[...]], axis=0)
    keys[rows_dev:nkeys] = dot(
        norm_rows(near).astype(BF16), wproj[:, half : 3 * half]
    ).astype(BF16)

    pairs = []

    def cross_pair(i):
        numerator, denominator = attend_pair(
            cross_query[:, 128 * i : 128 * (i + 1)],
            keys[:, 128 * i : 128 * (i + 1)],
            keys[:, half + 128 * i : half + 128 * (i + 1)],
            usable,
        )
        pairs.append((numerator / denominator).astype(BF16))

    npairs = half // 128
    for i in range(npairs):
        cross_pair(i)
        if i == 0:
            for copy in kv_x:
                copy.wait_recv()
            kv_s.append(send(slots(kvbuf, 1, nx - 1), slots(kvbuf, 2 * nx + 1, nx - 1), (sibling, mp)))
        if i == 1:
            for copy in kv_x2:
                copy.wait_recv()
            kv_s.append(send(slots(kvbuf, nx, nx), slots(kvbuf, 3 * nx, nx), (sibling, mp)))
    loads[4].wait()
    cross_out[...] = dot(jnp.concatenate(pairs, axis=1), wco[...]).astype(BF16)
    cross_move = send(cross_out, cross_in, (me, 1 - mp))

    for copy in q_z:
        copy.wait_recv()
    for copy in kv_s:
        copy.wait_recv()

    half_mod = lax.rem(iota((1, 128), 1), 64)

    def partials(queries):
        parts, dens = [], []
        for i in range(npairs):
            numerator, denominator = attend_pair(
                queries[:, 128 * i : 128 * (i + 1)],
                kvbuf[:, 128 * i : 128 * (i + 1)],
                kvbuf[:, half + 128 * i : half + 128 * (i + 1)],
                None,
            )
            parts.append(numerator)
            dens.append(denominator)
        packed = dens[0]
        for i in range(1, npairs):
            packed = jnp.where(half_mod >= 16 * i, dens[i], packed)
        return jnp.concatenate(parts + [packed], axis=1)

    rs_move = []
    quarter = nz // 4
    far = partials(qbuf[quarter * KEPT : (nz - quarter) * KEPT])
    rsout[quarter * KEPT : (nz - quarter) * KEPT] = far.astype(BF16)
    for k in far_first:
        if quarter <= k < nz - quarter:
            rs_move.append(send(slots(rsout, k, 1), slots(rsin, nz - k, 1), (zpeer[k], mp)))
    close = partials(
        jnp.concatenate([qbuf[(nz - quarter) * KEPT : nz * KEPT], qbuf[0 : quarter * KEPT]], axis=0)
    )
    rsout[(nz - quarter) * KEPT : nz * KEPT] = close[: quarter * KEPT].astype(BF16)
    rsout[0 : quarter * KEPT] = close[quarter * KEPT :].astype(BF16)
    for k in far_first:
        if not quarter <= k < nz - quarter:
            rs_move.append(send(slots(rsout, k, 1), slots(rsin, nz - k, 1), (zpeer[k], mp)))
    total = close[quarter * KEPT : (quarter + 1) * KEPT]

    cross_move.wait_recv()
    pruned = patches.astype(F32) + (cross_out[...].astype(F32) + cross_in[...].astype(F32))

    for copy in rs_move:
        copy.wait_recv()
    for k in range(1, nz):
        total = total + rsin[k * KEPT : (k + 1) * KEPT].astype(F32)
    low = iota((KEPT, 128), 1) < 64
    attention = []
    for i in range(npairs):
        first = total[:, half + 16 * i : half + 16 * i + 1]
        second = total[:, half + 64 + 16 * i : half + 64 + 16 * i + 1]
        attention.append(
            (total[:, 128 * i : 128 * (i + 1)] / jnp.where(low, first, second)).astype(BF16)
        )
    loads[5].wait()
    attn_out[...] = dot(jnp.concatenate(attention, axis=1), wo[...]).astype(BF16)
    attn_move = send(attn_out, attn_in, (me, 1 - mp))
    loads[6].wait()
    loads[7].wait()
    attn_move.wait_recv()
    hidden = kept + (attn_out[...].astype(F32) + attn_in[...].astype(F32))
    gated = jax.nn.gelu(dot(norm_rows(hidden).astype(BF16), wu[...]), approximate=True)
    down_out[...] = dot(gated.astype(BF16), wd[...]).astype(BF16)
    down_move = send(down_out, down_in, (me, 1 - mp))
    down_move.wait_recv()
    result[...] = (hidden + (down_out[...].astype(F32) + down_in[...].astype(F32))).astype(BF16)
    result_right = send(result.at[KEPT - EDGE : KEPT], left_result, (right, mp))
    result_left = send(result.at[0:EDGE], right_result, (left, mp))
    result_right.wait_recv()
    result_left.wait_recv()
    finished = jnp.concatenate([left_result[...], result[...], right_result[...]], axis=0)
    spread = dot_0(own_place, finished)
    out_ref[...] = jnp.where(kept_column, spread, pruned).astype(BF16)

    for copy in started:
        copy.wait_send()


def body(nx, nz, patches, keep_mask, segment, *weights):
    rows, width = patches.shape
    half = weights[0].shape[1]
    hidden = weights[6].shape[1]
    ntm = nx * nz * 4
    copies = 24 + 3 * (nx - 1) + 2 * (nz - 1)
    vmem = lambda *shape: pltpu.VMEM(shape, BF16)
    return pl.pallas_call(
        functools.partial(kernel, nx, nz),
        out_shape=jax.ShapeDtypeStruct((rows, width), BF16),
        in_specs=[pl.BlockSpec(memory_space=pltpu.VMEM)] * 3
        + [pl.BlockSpec(memory_space=pl.ANY)] * 8,
        out_specs=pl.BlockSpec(memory_space=pltpu.VMEM),
        scratch_shapes=[
            vmem(width, 4 * half),
            vmem(half, width),
            vmem(half, width),
            vmem(width, hidden),
            vmem(hidden, width),
            vmem(WINDOW, width),
            vmem(WINDOW, width),
            vmem(WINDOW, width),
            vmem(4 * nx * KEPT, 2 * half),
            vmem(nz * KEPT, half),
            vmem(nz * KEPT, half + 128),
            vmem(nz * KEPT, half + 128),
            vmem(rows + 2 * WINDOW, 2 * half),
            vmem(KEPT, width),
            vmem(KEPT, width),
            vmem(rows, width),
            vmem(rows, width),
            vmem(KEPT, width),
            vmem(KEPT, width),
            vmem(KEPT, width),
            vmem(EDGE, width),
            vmem(EDGE, width),
            pltpu.SemaphoreType.DMA((8,)),
            pltpu.SemaphoreType.DMA((copies,)),
            pltpu.SemaphoreType.DMA((copies,)),
        ],
        compiler_params=pltpu.CompilerParams(
            collective_id=0, has_side_effects=True, vmem_limit_bytes=48 * 1024 * 1024
        ),
    )(patches, keep_mask.reshape(ntm, rows), segment.reshape(ntm, rows), *weights)


def solution(mesh):
    placed = (
        P("tm", None),
        P(),
        P(),
        P(None, "mp"),
        P(None, "mp"),
        P(None, "mp"),
        P("mp", None),
        P(None, "mp"),
        P("mp", None),
        P(None, "mp"),
        P("mp", None),
    )
    ntm = mesh.shape["tm"]
    nx = 4 if ntm == 128 else 2
    return jax.shard_map(
        functools.partial(body, nx, ntm // (4 * nx)),
        mesh=mesh,
        in_specs=placed,
        out_specs=P("tm", None),
        check_vma=False,
    )
```

```python
import functools

import jax
import jax.numpy as jnp
from jax import lax
from jax.experimental import pallas as pl
from jax.experimental.pallas import tpu as pltpu
from jax.sharding import PartitionSpec as P

KEPT = 48
EDGE = 16
WINDOW = KEPT + 2 * EDGE
F32 = jnp.float32
BF16 = jnp.bfloat16


def norm_rows(values):
    values = values.astype(F32)
    center = values - jnp.mean(values, axis=-1, keepdims=True)
    return center * lax.rsqrt(jnp.mean(center * center, axis=-1, keepdims=True) + 1e-05)


def dot(a, b):
    return jnp.dot(a, b, preferred_element_type=F32)


def dot_t(a, b):
    return lax.dot_general(a, b, (((1,), (1,)), ((), ())), preferred_element_type=F32)


def dot_0(a, b):
    return lax.dot_general(a, b, (((0,), (0,)), ((), ())), preferred_element_type=F32)


def iota(shape, dim):
    return lax.broadcasted_iota(jnp.int32, shape, dim)


def attend_pair(queries, keys, values, usable):
    rows = queries.shape[0]
    low = iota((rows, 128), 1) < 64
    zero = jnp.zeros_like(queries)
    both = jnp.concatenate([jnp.where(low, queries, zero), jnp.where(low, zero, queries)], axis=0)
    weight = jnp.exp(dot_t(both, keys))
    if usable is not None:
        weight = jnp.where(usable, weight, 0.0)
    ones = jnp.ones((keys.shape[0], 128), BF16)
    total = dot(weight.astype(BF16), jnp.concatenate([values, ones], axis=1))
    numerator = jnp.where(low, total[:rows, :128], total[rows:, :128])
    denominator = jnp.where(low, total[:rows, 128:], total[rows:, 128:])
    return numerator, denominator


def kernel(
    nx,
    nz,
    patches_hbm,
    mask_hbm,
    seg_hbm,
    wq_hbm,
    wk_hbm,
    wv_hbm,
    wo_hbm,
    wcq_hbm,
    wco_hbm,
    wu_hbm,
    wd_hbm,
    out_ref,
    patches_ref,
    mask_ref,
    seg_ref,
    wproj,
    wo,
    wco,
    wu,
    wd,
    xwin,
    lwin,
    rwin,
    kvbuf,
    qbuf,
    rsout,
    rsin,
    acc,
    keys,
    attn_out,
    attn_in,
    cross_out,
    cross_in,
    down_out,
    down_in,
    edge_hidden,
    left_hidden,
    right_hidden,
    left_down,
    right_down,
    wsem,
    ssem,
    rsem,
):
    ntm = nx * nz * 4
    rows_dev, width = patches_hbm.shape
    half = wq_hbm.shape[1]
    me = lax.axis_index("tm")
    mp = lax.axis_index("mp")
    core = lax.rem(me, 2)
    yh = lax.rem(me // 2, 2)
    z = lax.rem(me // 4, nz)
    x = me // (4 * nz)
    sibling = (me + 1 - 2 * core, mp)
    ypart = me + 2 - 4 * yh
    right = lax.rem(me + 1, ntm)
    left = lax.rem(me + ntm - 1, ntm)
    right_side = (right, mp + core * (1 - 2 * mp))
    left_side = (left, mp + (1 - core) * (1 - 2 * mp))
    partner = (me, 1 - mp)
    zpeer = [(me + 4 * (lax.rem(z + k, nz) - z), mp) for k in range(nz)]
    xpeer = [(me + 4 * nz * (lax.rem(x + k, nx) - x), mp) for k in range(nx)]
    xypeer = [(ypart + 4 * nz * (lax.rem(x + k, nx) - x), mp) for k in range(nx)]
    neighbours = [(right, mp), (right, 1 - mp), (left, mp), (left, 1 - mp)]

    barrier = pltpu.get_barrier_semaphore()
    greeted = [sibling, partner] + neighbours + zpeer[1:] + xpeer[1:] + xypeer
    for target in greeted:
        pl.semaphore_signal(
            barrier, inc=1, device_id=target, device_id_type=pl.DeviceIdType.MESH
        )

    sources = [
        (mask_hbm, mask_ref),
        (patches_hbm, patches_ref),
        (seg_hbm, seg_ref),
        (wq_hbm, wproj.at[:, 0:half]),
        (wk_hbm, wproj.at[:, half : 2 * half]),
        (wv_hbm, wproj.at[:, 2 * half : 3 * half]),
        (wcq_hbm, wproj.at[:, 3 * half : 4 * half]),
        (wco_hbm, wco),
        (wo_hbm, wo),
        (wu_hbm, wu),
        (wd_hbm, wd),
    ]
    loads = []
    for i, (source, target) in enumerate(sources):
        load = pltpu.make_async_copy(source, target, wsem.at[i])
        load.start()
        loads.append(load)

    counter = [0]
    started = []

    def send(source, target, where):
        i = counter[0]
        counter[0] += 1
        copy = pltpu.make_async_remote_copy(
            src_ref=source,
            dst_ref=target,
            send_sem=ssem.at[i],
            recv_sem=rsem.at[i],
            device_id=where,
            device_id_type=pl.DeviceIdType.MESH,
        )
        copy.start()
        started.append(copy)
        return copy

    loads[0].wait()
    mask = mask_ref[...].astype(F32)
    place = iota(mask.shape, 0) * 128 + iota(mask.shape, 1)
    before = jnp.where(place < me * rows_dev, mask, 0.0)
    base = jnp.sum(jnp.sum(before, axis=1, keepdims=True), axis=0, keepdims=True)
    base = base - (KEPT * me).astype(F32)

    def run_of(ref, index):
        first = index * rows_dev // 128
        both = jnp.concatenate([ref[pl.ds(first, 1), :], ref[pl.ds(first + 1, 1), :]], axis=1)
        phase = lax.rem(index, 4)
        row = both[:, 0:rows_dev]
        for k in range(1, 4):
            row = jnp.where(phase == k, both[:, 32 * k : 32 * k + rows_dev], row)
        return row.astype(F32)

    own_mask = run_of(mask_ref, me)
    left_mask = jnp.where(me > 0, run_of(mask_ref, left), 0.0)
    right_mask = jnp.where(me < ntm - 1, run_of(mask_ref, right), 0.0)
    earlier = (iota((rows_dev, rows_dev), 0) < iota((rows_dev, rows_dev), 1)).astype(F32)
    earlier = earlier.astype(BF16)

    def window(mask_row, base_row):
        rank = dot(jnp.broadcast_to(mask_row, (16, rows_dev)).astype(BF16), earlier)[0:1]
        slot = jnp.where(mask_row > 0.5, rank + base_row + float(EDGE), -1.0)
        grid = iota((WINDOW, rows_dev), 0).astype(F32)
        return jnp.where(grid == slot, 1.0, 0.0).astype(BF16)

    own_place = window(own_mask, base)
    loads[1].wait()
    patches = patches_ref[...]
    xwin[...] = dot(own_place, patches).astype(BF16)

    pl.semaphore_wait(barrier, len(greeted))

    edge_right = send(xwin.at[KEPT + EDGE : WINDOW], lwin.at[KEPT + EDGE : WINDOW], right_side)
    edge_left = send(xwin.at[0:EDGE], rwin.at[0:EDGE], left_side)
    halo_right = send(xwin.at[0 : KEPT + EDGE], lwin.at[0 : KEPT + EDGE], right_side)
    halo_left = send(xwin.at[EDGE:WINDOW], rwin.at[EDGE:WINDOW], left_side)

    loads[2].wait()
    own_seg = run_of(seg_ref, me) + 1.0
    left_seg = run_of(seg_ref, left) + 1.0
    right_seg = run_of(seg_ref, right) + 1.0
    own_count = jnp.sum(own_mask, axis=1, keepdims=True)
    left_count = jnp.sum(left_mask, axis=1, keepdims=True)
    left_place = window(left_mask, base - left_count + float(KEPT))
    right_place = window(right_mask, base + own_count - float(KEPT))

    def key_segments(mask_place, seg_row):
        return dot_t(jnp.broadcast_to(seg_row, (16, rows_dev)).astype(BF16), mask_place)[0:1]

    key_seg = jnp.concatenate(
        [
            jnp.where(own_mask > 0.5, own_seg, 0.0),
            key_segments(left_place, left_seg),
            key_segments(right_place, right_seg),
        ],
        axis=1,
    )
    nkeys = rows_dev + 2 * WINDOW
    same = iota((rows_dev, rows_dev), 0) == iota((rows_dev, rows_dev), 1)
    seg_diag = jnp.where(same, own_seg, 0.0).astype(BF16)
    mask_diag = jnp.where(same, own_mask, 0.0).astype(BF16)
    query_seg = dot(seg_diag, jnp.ones((rows_dev, nkeys), BF16))
    usable = (query_seg == key_seg) | (
        iota((rows_dev, nkeys), 0) == iota((rows_dev, nkeys), 1)
    )
    usable = jnp.where(usable, 1.0, 0.0)
    usable = jnp.concatenate([usable, usable], axis=0) > 0.5
    kept_column = dot(mask_diag, jnp.ones((rows_dev, width), BF16)) > 0.5
    normed = norm_rows(patches).astype(BF16)

    edge_right.wait_recv()
    edge_left.wait_recv()
    own_rows = xwin[EDGE : EDGE + KEPT].astype(F32)
    kept = jnp.concatenate(
        [
            own_rows[:EDGE]
            + jnp.where(me > 0, lwin[WINDOW - EDGE : WINDOW].astype(F32), 0.0),
            own_rows[EDGE : KEPT - EDGE],
            own_rows[KEPT - EDGE :] + jnp.where(me < ntm - 1, rwin[0:EDGE].astype(F32), 0.0),
        ],
        axis=0,
    )
    for load in loads[3:6]:
        load.wait()
    qkv = dot(norm_rows(kept).astype(BF16), wproj[:, : 3 * half])
    qbuf[0:KEPT] = (qkv[:, :half].astype(BF16).astype(F32) * 0.125).astype(BF16)
    kvbuf[0:KEPT] = qkv[:, half:].astype(BF16)

    def slots(ref, first, count):
        return ref.at[first * KEPT : (first + count) * KEPT]

    own_kv, own_q = slots(kvbuf, 0, 1), slots(qbuf, 0, 1)
    far_first = sorted(range(1, nz), key=lambda k: -min(k, nz - k))
    far_x = sorted(range(nx), key=lambda k: -min(k, nx - k))
    q_z, kv_x, kv_xy, kv_s = [], [], [], []
    for n in range(max(nx, nz)):
        if n < nx:
            k = far_x[n]
            kv_xy.append(send(own_kv, slots(kvbuf, nx + (nx - k) % nx, 1), xypeer[k]))
        if n < nz - 1:
            k = far_first[n]
            q_z.append(send(own_q, slots(qbuf, nz - k, 1), zpeer[k]))
        if n < nx - 1:
            k = far_x[n]
            kv_x.append(send(own_kv, slots(kvbuf, nx - k, 1), xpeer[k]))
    kv_s.append(send(own_kv, slots(kvbuf, 2 * nx, 1), sibling))

    loads[6].wait()
    own_proj = dot(normed, wproj[:, half:])
    keys[0:rows_dev] = own_proj[:, : 2 * half].astype(BF16)
    cross_query = (own_proj[:, 2 * half :].astype(BF16).astype(F32) * 0.125).astype(BF16)

    halo_right.wait_recv()
    halo_left.wait_recv()
    near = jnp.concatenate([lwin[...], rwin[...]], axis=0)
    keys[rows_dev:nkeys] = dot(
        norm_rows(near).astype(BF16), wproj[:, half : 3 * half]
    ).astype(BF16)

    pairs = []

    def cross_pair(i):
        numerator, denominator = attend_pair(
            cross_query[:, 128 * i : 128 * (i + 1)],
            keys[:, 128 * i : 128 * (i + 1)],
            keys[:, half + 128 * i : half + 128 * (i + 1)],
            usable,
        )
        pairs.append((numerator / denominator).astype(BF16))

    npairs = half // 128
    for i in range(npairs):
        cross_pair(i)
    loads[7].wait()
    cross_out[...] = dot(jnp.concatenate(pairs, axis=1), wco[...]).astype(BF16)

    for copy in kv_x:
        copy.wait_recv()
    kv_s.append(send(slots(kvbuf, 1, nx - 1), slots(kvbuf, 2 * nx + 1, nx - 1), sibling))
    for copy in kv_xy:
        copy.wait_recv()
    kv_s.append(send(slots(kvbuf, nx, nx), slots(kvbuf, 3 * nx, nx), sibling))
    cross_move = send(cross_out, cross_in, partner)
    for copy in q_z:
        copy.wait_recv()

    half_mod = lax.rem(iota((1, 128), 1), 64)

    def partials(queries, first, last):
        parts, dens = [], []
        for i in range(npairs):
            numerator, denominator = attend_pair(
                queries[:, 128 * i : 128 * (i + 1)],
                kvbuf[first:last, 128 * i : 128 * (i + 1)],
                kvbuf[first:last, half + 128 * i : half + 128 * (i + 1)],
                None,
            )
            parts.append(numerator)
            dens.append(denominator)
        packed = dens[0]
        for i in range(1, npairs):
            packed = jnp.where(half_mod >= 16 * i, dens[i], packed)
        return jnp.concatenate(parts + [packed], axis=1)

    nkv = kvbuf.shape[0]
    acc[...] = partials(qbuf[...], 0, nkv // 2)
    for copy in kv_s:
        copy.wait_recv()
    rs_move = []
    near_far = nz // 4 * KEPT
    last = nz * KEPT - near_far
    far = acc[near_far:last] + partials(qbuf[near_far:last], nkv // 2, nkv)
    rsout[near_far:last] = far.astype(BF16)
    for k in far_first:
        if near_far <= k * KEPT < last:
            rs_move.append(send(slots(rsout, k, 1), slots(rsin, nz - k, 1), zpeer[k]))
    close = partials(
        jnp.concatenate([qbuf[last:], qbuf[:near_far]], axis=0), nkv // 2, nkv
    ) + jnp.concatenate([acc[last:], acc[:near_far]], axis=0)
    rsout[last:] = close[:near_far].astype(BF16)
    rsout[:near_far] = close[near_far:].astype(BF16)
    for k in far_first:
        if not near_far <= k * KEPT < last:
            rs_move.append(send(slots(rsout, k, 1), slots(rsin, nz - k, 1), zpeer[k]))
    total = close[near_far : near_far + KEPT]

    cross_move.wait_recv()
    pruned = patches.astype(F32) + (cross_out[...].astype(F32) + cross_in[...].astype(F32))

    for copy in rs_move:
        copy.wait_recv()
    for k in range(1, nz):
        total = total + rsin[k * KEPT : (k + 1) * KEPT].astype(F32)
    low = iota((KEPT, 128), 1) < 64
    attention = []
    for i in range(npairs):
        first = total[:, half + 16 * i : half + 16 * i + 1]
        second = total[:, half + 64 + 16 * i : half + 64 + 16 * i + 1]
        attention.append(
            (total[:, 128 * i : 128 * (i + 1)] / jnp.where(low, first, second)).astype(BF16)
        )
    loads[8].wait()
    attn_out[...] = dot(jnp.concatenate(attention, axis=1), wo[...]).astype(BF16)
    attn_move = send(attn_out, attn_in, partner)
    loads[9].wait()
    loads[10].wait()
    attn_move.wait_recv()
    hidden = kept + (attn_out[...].astype(F32) + attn_in[...].astype(F32))
    edge_hidden[0:EDGE] = hidden[:EDGE]
    edge_hidden[EDGE : 2 * EDGE] = hidden[KEPT - EDGE :]
    hidden_right = send(edge_hidden.at[EDGE : 2 * EDGE], left_hidden, right_side)
    hidden_left = send(edge_hidden.at[0:EDGE], right_hidden, left_side)
    gated = jax.nn.gelu(dot(norm_rows(hidden).astype(BF16), wu[...]), approximate=True)
    down_out[...] = dot(gated.astype(BF16), wd[...]).astype(BF16)
    ends = []
    for n, side in enumerate((mp, 1 - mp)):
        there = slice(n * EDGE, (n + 1) * EDGE)
        ends.append(send(down_out.at[KEPT - EDGE : KEPT], left_down.at[there], (right, side)))
        ends.append(send(down_out.at[0:EDGE], right_down.at[there], (left, side)))
    down_move = send(down_out, down_in, partner)
    hidden_right.wait_recv()
    hidden_left.wait_recv()
    down_move.wait_recv()
    own_result = hidden + (down_out[...].astype(F32) + down_in[...].astype(F32))
    for copy in ends:
        copy.wait_recv()

    def edge_result(base_ref, parts_ref):
        parts = parts_ref[...].astype(F32)
        return base_ref[...] + (parts[:EDGE] + parts[EDGE:])

    finished = jnp.concatenate(
        [
            edge_result(left_hidden, left_down),
            own_result,
            edge_result(right_hidden, right_down),
        ],
        axis=0,
    )
    spread = dot_0(own_place, finished.astype(BF16))
    out_ref[...] = jnp.where(kept_column, spread, pruned).astype(BF16)

    for copy in started:
        copy.wait_send()


def body(nx, nz, patches, keep_mask, segment, *weights):
    rows, width = patches.shape
    half = weights[0].shape[1]
    hidden = weights[6].shape[1]
    ntm = nx * nz * 4
    copies = 17 + 2 * nx + 2 * (nz - 1)
    vmem = lambda *shape: pltpu.VMEM(shape, BF16)
    return pl.pallas_call(
        functools.partial(kernel, nx, nz),
        out_shape=jax.ShapeDtypeStruct((rows, width), BF16),
        in_specs=[pl.BlockSpec(memory_space=pl.ANY)] * 11,
        out_specs=pl.BlockSpec(memory_space=pltpu.VMEM),
        scratch_shapes=[
            vmem(rows, width),
            pltpu.VMEM((ntm * rows // 128, 128), jnp.int32),
            pltpu.VMEM((ntm * rows // 128, 128), jnp.int32),
            vmem(width, 4 * half),
            vmem(half, width),
            vmem(half, width),
            vmem(width, hidden),
            vmem(hidden, width),
            vmem(WINDOW, width),
            vmem(WINDOW, width),
            vmem(WINDOW, width),
            vmem(4 * nx * KEPT, 2 * half),
            vmem(nz * KEPT, half),
            vmem(nz * KEPT, half + 128),
            vmem(nz * KEPT, half + 128),
            pltpu.VMEM((nz * KEPT, half + 128), F32),
            vmem(rows + 2 * WINDOW, 2 * half),
            vmem(KEPT, width),
            vmem(KEPT, width),
            vmem(rows, width),
            vmem(rows, width),
            vmem(KEPT, width),
            vmem(KEPT, width),
            pltpu.VMEM((2 * EDGE, width), F32),
            pltpu.VMEM((EDGE, width), F32),
            pltpu.VMEM((EDGE, width), F32),
            vmem(2 * EDGE, width),
            vmem(2 * EDGE, width),
            pltpu.SemaphoreType.DMA((11,)),
            pltpu.SemaphoreType.DMA((copies,)),
            pltpu.SemaphoreType.DMA((copies,)),
        ],
        compiler_params=pltpu.CompilerParams(
            collective_id=0, has_side_effects=True, vmem_limit_bytes=60 * 1024 * 1024
        ),
    )(patches, keep_mask.reshape(-1, 128), segment.reshape(-1, 128), *weights)


def solution(mesh):
    placed = (
        P("tm", None),
        P(),
        P(),
        P(None, "mp"),
        P(None, "mp"),
        P(None, "mp"),
        P("mp", None),
        P(None, "mp"),
        P("mp", None),
        P(None, "mp"),
        P("mp", None),
    )
    ntm = mesh.shape["tm"]
    nx = 4 if ntm == 128 else 2
    return jax.shard_map(
        functools.partial(body, nx, ntm // (4 * nx)),
        mesh=mesh,
        in_specs=placed,
        out_specs=P("tm", None),
        check_vma=False,
    )
```

```python
import functools

import jax
import jax.numpy as jnp
from jax import lax
from jax.experimental import pallas as pl
from jax.experimental.pallas import tpu as pltpu
from jax.sharding import PartitionSpec as P

KEPT = 48
EDGE = 16
WINDOW = KEPT + 2 * EDGE
F32 = jnp.float32
BF16 = jnp.bfloat16


def norm_rows(values):
    values = values.astype(F32)
    center = values - jnp.mean(values, axis=-1, keepdims=True)
    return center * lax.rsqrt(jnp.mean(center * center, axis=-1, keepdims=True) + 1e-05)


def dot(a, b):
    return jnp.dot(a, b, preferred_element_type=F32)


def dot_t(a, b):
    return lax.dot_general(a, b, (((1,), (1,)), ((), ())), preferred_element_type=F32)


def dot_0(a, b):
    return lax.dot_general(a, b, (((0,), (0,)), ((), ())), preferred_element_type=F32)


def iota(shape, dim):
    return lax.broadcasted_iota(jnp.int32, shape, dim)


def attend_pair(queries, keys, values, usable):
    rows = queries.shape[0]
    low = iota((rows, 128), 1) < 64
    zero = jnp.zeros_like(queries)
    both = jnp.concatenate([jnp.where(low, queries, zero), jnp.where(low, zero, queries)], axis=0)
    weight = jnp.exp(dot_t(both, keys))
    if usable is not None:
        weight = jnp.where(usable, weight, 0.0)
    ones = jnp.ones((keys.shape[0], 128), BF16)
    total = dot(weight.astype(BF16), jnp.concatenate([values, ones], axis=1))
    numerator = jnp.where(low, total[:rows, :128], total[rows:, :128])
    denominator = jnp.where(low, total[:rows, 128:], total[rows:, 128:])
    return numerator, denominator


def kernel(
    nx,
    nz,
    patches_hbm,
    mask_hbm,
    seg_hbm,
    wq_hbm,
    wk_hbm,
    wv_hbm,
    wo_hbm,
    wcq_hbm,
    wco_hbm,
    wu_hbm,
    wd_hbm,
    out_ref,
    patches_ref,
    mask_ref,
    seg_ref,
    wproj,
    wo,
    wco,
    wu,
    wd,
    xwin,
    lwin,
    rwin,
    kvbuf,
    qbuf,
    rsout,
    rsin,
    keys,
    attn_out,
    attn_in,
    cross_out,
    cross_in,
    down_out,
    down_in,
    edge_hidden,
    left_hidden,
    right_hidden,
    left_down,
    right_down,
    wsem,
    ssem,
    rsem,
):
    ntm = nx * nz * 4
    rows_dev, width = patches_hbm.shape
    half = wq_hbm.shape[1]
    me = lax.axis_index("tm")
    mp = lax.axis_index("mp")
    core = lax.rem(me, 2)
    yh = lax.rem(me // 2, 2)
    z = lax.rem(me // 4, nz)
    x = me // (4 * nz)
    sibling = (me + 1 - 2 * core, mp)
    ypart = me + 2 - 4 * yh
    right = lax.rem(me + 1, ntm)
    left = lax.rem(me + ntm - 1, ntm)
    right_side = (right, mp + core * (1 - 2 * mp))
    left_side = (left, mp + (1 - core) * (1 - 2 * mp))
    partner = (me, 1 - mp)
    zpeer = [(me + 4 * (lax.rem(z + k, nz) - z), mp) for k in range(nz)]
    xpeer = [(me + 4 * nz * (lax.rem(x + k, nx) - x), mp) for k in range(nx)]
    xypeer = [(ypart + 4 * nz * (lax.rem(x + k, nx) - x), mp) for k in range(nx)]
    neighbours = [(right, mp), (right, 1 - mp), (left, mp), (left, 1 - mp)]

    barrier = pltpu.get_barrier_semaphore()
    greeted = [sibling, partner] + neighbours + zpeer[1:] + xpeer[1:] + xypeer
    for target in greeted:
        pl.semaphore_signal(
            barrier, inc=1, device_id=target, device_id_type=pl.DeviceIdType.MESH
        )

    sources = [
        (mask_hbm, mask_ref),
        (patches_hbm, patches_ref),
        (seg_hbm, seg_ref),
        (wq_hbm, wproj.at[:, 0:half]),
        (wk_hbm, wproj.at[:, half : 2 * half]),
        (wv_hbm, wproj.at[:, 2 * half : 3 * half]),
        (wcq_hbm, wproj.at[:, 3 * half : 4 * half]),
        (wco_hbm, wco),
        (wo_hbm, wo),
        (wu_hbm, wu),
        (wd_hbm, wd),
    ]
    loads = []
    for i, (source, target) in enumerate(sources):
        load = pltpu.make_async_copy(source, target, wsem.at[i])
        load.start()
        loads.append(load)

    counter = [0]
    started = []

    def send(source, target, where):
        i = counter[0]
        counter[0] += 1
        copy = pltpu.make_async_remote_copy(
            src_ref=source,
            dst_ref=target,
            send_sem=ssem.at[i],
            recv_sem=rsem.at[i],
            device_id=where,
            device_id_type=pl.DeviceIdType.MESH,
        )
        copy.start()
        started.append(copy)
        return copy

    loads[0].wait()
    mask = mask_ref[...].astype(F32)
    place = iota(mask.shape, 0) * 128 + iota(mask.shape, 1)
    before = jnp.where(place < me * rows_dev, mask, 0.0)
    base = jnp.sum(jnp.sum(before, axis=1, keepdims=True), axis=0, keepdims=True)
    base = base - (KEPT * me).astype(F32)

    def run_of(ref, index):
        first = index * rows_dev // 128
        both = jnp.concatenate([ref[pl.ds(first, 1), :], ref[pl.ds(first + 1, 1), :]], axis=1)
        phase = lax.rem(index, 4)
        row = both[:, 0:rows_dev]
        for k in range(1, 4):
            row = jnp.where(phase == k, both[:, 32 * k : 32 * k + rows_dev], row)
        return row.astype(F32)

    own_mask = run_of(mask_ref, me)
    left_mask = jnp.where(me > 0, run_of(mask_ref, left), 0.0)
    right_mask = jnp.where(me < ntm - 1, run_of(mask_ref, right), 0.0)
    earlier = (iota((rows_dev, rows_dev), 0) < iota((rows_dev, rows_dev), 1)).astype(F32)
    earlier = earlier.astype(BF16)

    def window(mask_row, base_row):
        rank = dot(jnp.broadcast_to(mask_row, (16, rows_dev)).astype(BF16), earlier)[0:1]
        slot = jnp.where(mask_row > 0.5, rank + base_row + float(EDGE), -1.0)
        grid = iota((WINDOW, rows_dev), 0).astype(F32)
        return jnp.where(grid == slot, 1.0, 0.0).astype(BF16)

    own_place = window(own_mask, base)
    loads[1].wait()
    patches = patches_ref[...]
    xwin[...] = dot(own_place, patches).astype(BF16)

    pl.semaphore_wait(barrier, len(greeted))

    edge_right = send(xwin.at[KEPT + EDGE : WINDOW], lwin.at[KEPT + EDGE : WINDOW], right_side)
    edge_left = send(xwin.at[0:EDGE], rwin.at[0:EDGE], left_side)
    halo_right = send(xwin.at[0 : KEPT + EDGE], lwin.at[0 : KEPT + EDGE], right_side)
    halo_left = send(xwin.at[EDGE:WINDOW], rwin.at[EDGE:WINDOW], left_side)

    loads[2].wait()
    own_seg = run_of(seg_ref, me) + 1.0
    left_seg = run_of(seg_ref, left) + 1.0
    right_seg = run_of(seg_ref, right) + 1.0
    own_count = jnp.sum(own_mask, axis=1, keepdims=True)
    left_count = jnp.sum(left_mask, axis=1, keepdims=True)
    left_place = window(left_mask, base - left_count + float(KEPT))
    right_place = window(right_mask, base + own_count - float(KEPT))

    def key_segments(mask_place, seg_row):
        return dot_t(jnp.broadcast_to(seg_row, (16, rows_dev)).astype(BF16), mask_place)[0:1]

    key_seg = jnp.concatenate(
        [
            jnp.where(own_mask > 0.5, own_seg, 0.0),
            key_segments(left_place, left_seg),
            key_segments(right_place, right_seg),
        ],
        axis=1,
    )
    nkeys = rows_dev + 2 * WINDOW
    same = iota((rows_dev, rows_dev), 0) == iota((rows_dev, rows_dev), 1)
    seg_diag = jnp.where(same, own_seg, 0.0).astype(BF16)
    mask_diag = jnp.where(same, own_mask, 0.0).astype(BF16)
    query_seg = dot(seg_diag, jnp.ones((rows_dev, nkeys), BF16))
    usable = (query_seg == key_seg) | (
        iota((rows_dev, nkeys), 0) == iota((rows_dev, nkeys), 1)
    )
    usable = jnp.where(usable, 1.0, 0.0)
    usable = jnp.concatenate([usable, usable], axis=0) > 0.5
    kept_column = dot(mask_diag, jnp.ones((rows_dev, width), BF16)) > 0.5
    normed = norm_rows(patches).astype(BF16)

    edge_right.wait_recv()
    edge_left.wait_recv()
    own_rows = xwin[EDGE : EDGE + KEPT].astype(F32)
    kept = jnp.concatenate(
        [
            own_rows[:EDGE]
            + jnp.where(me > 0, lwin[WINDOW - EDGE : WINDOW].astype(F32), 0.0),
            own_rows[EDGE : KEPT - EDGE],
            own_rows[KEPT - EDGE :] + jnp.where(me < ntm - 1, rwin[0:EDGE].astype(F32), 0.0),
        ],
        axis=0,
    )
    for load in loads[3:6]:
        load.wait()
    qkv = dot(norm_rows(kept).astype(BF16), wproj[:, : 3 * half])
    queries = (qkv[:, :half].astype(BF16).astype(F32) * 0.125).astype(BF16)
    kept_kv = qkv[:, half:].astype(BF16)
    npairs = half // 128
    nkv, nq = 4 * nx * KEPT, nz * KEPT
    for p in range(npairs):
        lanes = slice(128 * p, 128 * (p + 1))
        qbuf[p * nq : p * nq + KEPT] = queries[:, lanes]
        kvbuf[p * nkv : p * nkv + KEPT, :128] = kept_kv[:, :half][:, lanes]
        kvbuf[p * nkv : p * nkv + KEPT, 128:] = kept_kv[:, half:][:, lanes]

    def kv_slots(p, first, count):
        return kvbuf.at[p * nkv + first * KEPT : p * nkv + (first + count) * KEPT]

    def q_slot(p, k):
        return qbuf.at[p * nq + k * KEPT : p * nq + (k + 1) * KEPT]

    far_first = sorted(range(1, nz), key=lambda k: -min(k, nz - k))
    far_x = sorted(range(nx), key=lambda k: -min(k, nx - k))
    q_z, kv_x, kv_xy, kv_s = [], [], [], []
    for p in range(npairs):
        q_z.append([])
        kv_x.append([])
        kv_xy.append([])
        own_kv = kv_slots(p, 0, 1)
        for n in range(max(nx, nz)):
            if n < nx:
                k = far_x[n]
                kv_xy[p].append(send(own_kv, kv_slots(p, nx + (nx - k) % nx, 1), xypeer[k]))
            if n < nz - 1:
                k = far_first[n]
                q_z[p].append(send(q_slot(p, 0), q_slot(p, nz - k), zpeer[k]))
            if n < nx - 1:
                k = far_x[n]
                kv_x[p].append(send(own_kv, kv_slots(p, nx - k, 1), xpeer[k]))
        kv_s.append([send(own_kv, kv_slots(p, 2 * nx, 1), sibling)])

    loads[6].wait()
    own_proj = dot(normed, wproj[:, half:])
    keys[0:rows_dev] = own_proj[:, : 2 * half].astype(BF16)
    cross_query = (own_proj[:, 2 * half :].astype(BF16).astype(F32) * 0.125).astype(BF16)

    halo_right.wait_recv()
    halo_left.wait_recv()
    near = jnp.concatenate([lwin[...], rwin[...]], axis=0)
    keys[rows_dev:nkeys] = dot(
        norm_rows(near).astype(BF16), wproj[:, half : 3 * half]
    ).astype(BF16)

    pairs = []

    def cross_pair(i):
        numerator, denominator = attend_pair(
            cross_query[:, 128 * i : 128 * (i + 1)],
            keys[:, 128 * i : 128 * (i + 1)],
            keys[:, half + 128 * i : half + 128 * (i + 1)],
            usable,
        )
        pairs.append((numerator / denominator).astype(BF16))

    for i in range(npairs):
        cross_pair(i)
    loads[7].wait()
    cross_out[...] = dot(jnp.concatenate(pairs, axis=1), wco[...]).astype(BF16)

    half_mod = lax.rem(iota((1, 128), 1), 64)
    block = npairs * KEPT + 16
    head_lane = 64 * lax.rem(iota((16, 128), 0), 2) + 16 * (iota((16, 128), 0) // 2)
    pick = jnp.where(iota((16, 128), 1) == head_lane, 1.0, 0.0)
    pick = jnp.where(iota((16, 128), 0) < 2 * npairs, pick, 0.0).astype(BF16)
    totals, rs_move, packed = [], [], None
    for p in range(npairs):
        for copy in kv_x[p]:
            copy.wait_recv()
        kv_s[p].append(send(kv_slots(p, 1, nx - 1), kv_slots(p, 2 * nx + 1, nx - 1), sibling))
        for copy in kv_xy[p]:
            copy.wait_recv()
        kv_s[p].append(send(kv_slots(p, nx, nx), kv_slots(p, 3 * nx, nx), sibling))
        if p == npairs - 1:
            cross_move = send(cross_out, cross_in, partner)
        for copy in q_z[p]:
            copy.wait_recv()
        ring = qbuf[p * nq : (p + 1) * nq]
        first = slice(p * nkv, p * nkv + nkv // 2)
        second = slice(p * nkv + nkv // 2, (p + 1) * nkv)
        num, den = attend_pair(ring, kvbuf[first, :128], kvbuf[first, 128:], None)
        for copy in kv_s[p]:
            copy.wait_recv()
        num2, den2 = attend_pair(ring, kvbuf[second, :128], kvbuf[second, 128:], None)
        num, den = num + num2, den + den2
        packed = den if p == 0 else jnp.where(half_mod >= 16 * p, den, packed)
        totals.append(num[:KEPT])
        num = num.astype(BF16)
        for k in far_first + [0]:
            rows = slice(k * KEPT, (k + 1) * KEPT)
            there = k * block + p * KEPT
            count = KEPT
            if k:
                rsout[there : there + KEPT] = num[rows]
            if p == npairs - 1:
                own = jnp.concatenate([packed[rows], jnp.zeros((128 - KEPT, 128), F32)], axis=0)
                by_head = dot_t(pick, own.astype(BF16))
                count = KEPT + 16
                if k:
                    rsout[there + KEPT : there + count] = by_head.astype(BF16)
                else:
                    totals.append(by_head)
            if k:
                back = (nz - k) * block + p * KEPT
                rs_move.append(
                    send(rsout.at[there : there + count], rsin.at[back : back + count], zpeer[k])
                )

    cross_move.wait_recv()
    pruned = patches.astype(F32) + (cross_out[...].astype(F32) + cross_in[...].astype(F32))

    for copy in rs_move:
        copy.wait_recv()
    for p in range(npairs + 1):
        for k in range(1, nz):
            there = k * block + p * KEPT
            totals[p] += rsin[there : there + totals[p].shape[0]].astype(F32)
    by_head = totals[npairs]
    inverse = jnp.where(by_head > 0.0, 1.0 / by_head, 0.0)
    coarse = inverse.astype(BF16)
    fine = (inverse - coarse.astype(F32)).astype(BF16)
    widen = jnp.where(iota((16, half), 1) // 64 == iota((16, half), 0), 1.0, 0.0).astype(BF16)
    inverse = (dot_0(coarse, widen) + dot_0(fine, widen))[:KEPT]
    attention = [
        (totals[p] * inverse[:, 128 * p : 128 * (p + 1)]).astype(BF16) for p in range(npairs)
    ]
    loads[8].wait()
    attn_out[...] = dot(jnp.concatenate(attention, axis=1), wo[...]).astype(BF16)
    attn_move = send(attn_out, attn_in, partner)
    loads[9].wait()
    loads[10].wait()
    attn_move.wait_recv()
    hidden = kept + (attn_out[...].astype(F32) + attn_in[...].astype(F32))
    edge_hidden[0:EDGE] = hidden[:EDGE]
    edge_hidden[EDGE : 2 * EDGE] = hidden[KEPT - EDGE :]
    hidden_right = send(edge_hidden.at[EDGE : 2 * EDGE], left_hidden, right_side)
    hidden_left = send(edge_hidden.at[0:EDGE], right_hidden, left_side)
    gated = jax.nn.gelu(dot(norm_rows(hidden).astype(BF16), wu[...]), approximate=True)
    down_out[...] = dot(gated.astype(BF16), wd[...]).astype(BF16)
    ends = []
    for n, side in enumerate((mp, 1 - mp)):
        there = slice(n * EDGE, (n + 1) * EDGE)
        ends.append(send(down_out.at[KEPT - EDGE : KEPT], left_down.at[there], (right, side)))
        ends.append(send(down_out.at[0:EDGE], right_down.at[there], (left, side)))
    down_move = send(down_out, down_in, partner)
    hidden_right.wait_recv()
    hidden_left.wait_recv()
    down_move.wait_recv()
    own_result = hidden + (down_out[...].astype(F32) + down_in[...].astype(F32))
    for copy in ends:
        copy.wait_recv()

    def edge_result(base_ref, parts_ref):
        parts = parts_ref[...].astype(F32)
        return base_ref[...] + (parts[:EDGE] + parts[EDGE:])

    finished = jnp.concatenate(
        [
            edge_result(left_hidden, left_down),
            own_result,
            edge_result(right_hidden, right_down),
        ],
        axis=0,
    )
    spread = dot_0(own_place, finished.astype(BF16))
    out_ref[...] = jnp.where(kept_column, spread, pruned).astype(BF16)

    for copy in started:
        copy.wait_send()


def body(nx, nz, patches, keep_mask, segment, *weights):
    rows, width = patches.shape
    half = weights[0].shape[1]
    hidden = weights[6].shape[1]
    ntm = nx * nz * 4
    npairs = half // 128
    copies = 14 + npairs * (2 * nx + 2 + 2 * (nz - 1))
    vmem = lambda *shape: pltpu.VMEM(shape, BF16)
    return pl.pallas_call(
        functools.partial(kernel, nx, nz),
        out_shape=pltpu.VMEM((rows, width), BF16),
        in_specs=[pl.BlockSpec(memory_space=pl.ANY)] * 11,
        out_specs=pl.BlockSpec(memory_space=pltpu.VMEM),
        scratch_shapes=[
            vmem(rows, width),
            pltpu.VMEM((ntm * rows // 128, 128), jnp.int32),
            pltpu.VMEM((ntm * rows // 128, 128), jnp.int32),
            vmem(width, 4 * half),
            vmem(half, width),
            vmem(half, width),
            vmem(width, hidden),
            vmem(hidden, width),
            vmem(WINDOW, width),
            vmem(WINDOW, width),
            vmem(WINDOW, width),
            vmem(npairs * 4 * nx * KEPT, 256),
            vmem(npairs * nz * KEPT, 128),
            vmem(nz * (npairs * KEPT + 16), 128),
            vmem(nz * (npairs * KEPT + 16), 128),
            vmem(rows + 2 * WINDOW, 2 * half),
            vmem(KEPT, width),
            vmem(KEPT, width),
            vmem(rows, width),
            vmem(rows, width),
            vmem(KEPT, width),
            vmem(KEPT, width),
            pltpu.VMEM((2 * EDGE, width), F32),
            pltpu.VMEM((EDGE, width), F32),
            pltpu.VMEM((EDGE, width), F32),
            vmem(2 * EDGE, width),
            vmem(2 * EDGE, width),
            pltpu.SemaphoreType.DMA((11,)),
            pltpu.SemaphoreType.DMA((copies,)),
            pltpu.SemaphoreType.DMA((copies,)),
        ],
        compiler_params=pltpu.CompilerParams(
            collective_id=0, has_side_effects=True, vmem_limit_bytes=60 * 1024 * 1024
        ),
    )(patches, keep_mask.reshape(-1, 128), segment.reshape(-1, 128), *weights)


def solution(mesh):
    placed = (
        P("tm", None),
        P(),
        P(),
        P(None, "mp"),
        P(None, "mp"),
        P(None, "mp"),
        P("mp", None),
        P(None, "mp"),
        P("mp", None),
        P(None, "mp"),
        P("mp", None),
    )
    ntm = mesh.shape["tm"]
    nx = 4 if ntm == 128 else 2
    return jax.shard_map(
        functools.partial(body, nx, ntm // (4 * nx)),
        mesh=mesh,
        in_specs=placed,
        out_specs=P("tm", None),
        check_vma=False,
    )
```

```python
import functools

import jax
import jax.numpy as jnp
from jax import lax
from jax.experimental import pallas as pl
from jax.experimental.pallas import tpu as pltpu
from jax.sharding import PartitionSpec as P

KEPT = 48
EDGE = 16
WINDOW = KEPT + 2 * EDGE
F32 = jnp.float32
BF16 = jnp.bfloat16


def norm_rows(values):
    values = values.astype(F32)
    center = values - jnp.mean(values, axis=-1, keepdims=True)
    return center * lax.rsqrt(jnp.mean(center * center, axis=-1, keepdims=True) + 1e-05)


def dot(a, b):
    return jnp.dot(a, b, preferred_element_type=F32)


def dot_t(a, b):
    return lax.dot_general(a, b, (((1,), (1,)), ((), ())), preferred_element_type=F32)


def dot_0(a, b):
    return lax.dot_general(a, b, (((0,), (0,)), ((), ())), preferred_element_type=F32)


def iota(shape, dim):
    return lax.broadcasted_iota(jnp.int32, shape, dim)


def attend_pair(queries, keys, values, usable):
    rows = queries.shape[0]
    low = iota((rows, 128), 1) < 64
    zero = jnp.zeros_like(queries)
    both = jnp.concatenate([jnp.where(low, queries, zero), jnp.where(low, zero, queries)], axis=0)
    weight = jnp.exp(dot_t(both, keys))
    if usable is not None:
        weight = jnp.where(usable, weight, 0.0)
    ones = jnp.ones((keys.shape[0], 128), BF16)
    total = dot(weight.astype(BF16), jnp.concatenate([values, ones], axis=1))
    numerator = jnp.where(low, total[:rows, :128], total[rows:, :128])
    denominator = jnp.where(low, total[:rows, 128:], total[rows:, 128:])
    return numerator, denominator


def kernel(
    nx,
    nz,
    patches_hbm,
    mask_hbm,
    seg_hbm,
    wq_hbm,
    wk_hbm,
    wv_hbm,
    wo_hbm,
    wcq_hbm,
    wco_hbm,
    wu_hbm,
    wd_hbm,
    out_ref,
    patches_ref,
    mask_ref,
    seg_ref,
    wproj,
    wo,
    wco,
    wu,
    wd,
    xwin,
    lwin,
    rwin,
    kvbuf,
    qbuf,
    rsout,
    rsin,
    keys,
    attn_out,
    attn_in,
    cross_out,
    cross_in,
    down_out,
    down_in,
    edge_hidden,
    left_hidden,
    right_hidden,
    left_down,
    right_down,
    wsem,
    ssem,
    rsem,
):
    ntm = nx * nz * 4
    rows_dev, width = patches_hbm.shape
    half = wq_hbm.shape[1]
    me = lax.axis_index("tm")
    mp = lax.axis_index("mp")
    core = lax.rem(me, 2)
    yh = lax.rem(me // 2, 2)
    z = lax.rem(me // 4, nz)
    x = me // (4 * nz)
    sibling = (me + 1 - 2 * core, mp)
    ypart = me + 2 - 4 * yh
    right = lax.rem(me + 1, ntm)
    left = lax.rem(me + ntm - 1, ntm)
    right_side = (right, mp + core * (1 - 2 * mp))
    left_side = (left, mp + (1 - core) * (1 - 2 * mp))
    partner = (me, 1 - mp)
    zpeer = [(me + 4 * (lax.rem(z + k, nz) - z), mp) for k in range(nz)]
    xpeer = [(me + 4 * nz * (lax.rem(x + k, nx) - x), mp) for k in range(nx)]
    xypeer = [(ypart + 4 * nz * (lax.rem(x + k, nx) - x), mp) for k in range(nx)]
    neighbours = [(right, mp), (right, 1 - mp), (left, mp), (left, 1 - mp)]

    barrier = pltpu.get_barrier_semaphore()
    greeted = [sibling, partner] + neighbours + zpeer[1:] + xpeer[1:] + xypeer
    for target in greeted:
        pl.semaphore_signal(
            barrier, inc=1, device_id=target, device_id_type=pl.DeviceIdType.MESH
        )

    sources = [
        (mask_hbm, mask_ref),
        (patches_hbm, patches_ref),
        (seg_hbm, seg_ref),
        (wq_hbm, wproj.at[:, 0:half]),
        (wk_hbm, wproj.at[:, half : 2 * half]),
        (wv_hbm, wproj.at[:, 2 * half : 3 * half]),
        (wcq_hbm, wproj.at[:, 3 * half : 4 * half]),
        (wco_hbm, wco),
        (wo_hbm, wo),
        (wu_hbm, wu),
        (wd_hbm, wd),
    ]
    loads = []
    for i, (source, target) in enumerate(sources):
        load = pltpu.make_async_copy(source, target, wsem.at[i])
        load.start()
        loads.append(load)

    counter = [0]
    started = []

    def send(source, target, where):
        i = counter[0]
        counter[0] += 1
        copy = pltpu.make_async_remote_copy(
            src_ref=source,
            dst_ref=target,
            send_sem=ssem.at[i],
            recv_sem=rsem.at[i],
            device_id=where,
            device_id_type=pl.DeviceIdType.MESH,
        )
        copy.start()
        started.append(copy)
        return copy

    loads[0].wait()
    mask = mask_ref[...].astype(F32)
    place = iota(mask.shape, 0) * 128 + iota(mask.shape, 1)
    before = jnp.where(place < me * rows_dev, mask, 0.0)
    base = jnp.sum(jnp.sum(before, axis=1, keepdims=True), axis=0, keepdims=True)
    base = base - (KEPT * me).astype(F32)

    def run_of(ref, index):
        first = index * rows_dev // 128
        both = jnp.concatenate([ref[pl.ds(first, 1), :], ref[pl.ds(first + 1, 1), :]], axis=1)
        phase = lax.rem(index, 4)
        row = both[:, 0:rows_dev]
        for k in range(1, 4):
            row = jnp.where(phase == k, both[:, 32 * k : 32 * k + rows_dev], row)
        return row.astype(F32)

    own_mask = run_of(mask_ref, me)
    left_mask = jnp.where(me > 0, run_of(mask_ref, left), 0.0)
    right_mask = jnp.where(me < ntm - 1, run_of(mask_ref, right), 0.0)
    earlier = (iota((rows_dev, rows_dev), 0) < iota((rows_dev, rows_dev), 1)).astype(F32)
    earlier = earlier.astype(BF16)

    def window(mask_row, base_row):
        rank = dot(jnp.broadcast_to(mask_row, (16, rows_dev)).astype(BF16), earlier)[0:1]
        slot = jnp.where(mask_row > 0.5, rank + base_row + float(EDGE), -1.0)
        grid = iota((WINDOW, rows_dev), 0).astype(F32)
        return jnp.where(grid == slot, 1.0, 0.0).astype(BF16)

    own_place = window(own_mask, base)
    loads[1].wait()
    patches = patches_ref[...]
    xwin[...] = dot(own_place, patches).astype(BF16)

    pl.semaphore_wait(barrier, len(greeted))

    edge_right = send(xwin.at[KEPT + EDGE : WINDOW], lwin.at[KEPT + EDGE : WINDOW], right_side)
    edge_left = send(xwin.at[0:EDGE], rwin.at[0:EDGE], left_side)
    halo_right = send(xwin.at[0 : KEPT + EDGE], lwin.at[0 : KEPT + EDGE], right_side)
    halo_left = send(xwin.at[EDGE:WINDOW], rwin.at[EDGE:WINDOW], left_side)

    loads[2].wait()
    own_seg = run_of(seg_ref, me) + 1.0
    left_seg = run_of(seg_ref, left) + 1.0
    right_seg = run_of(seg_ref, right) + 1.0
    own_count = jnp.sum(own_mask, axis=1, keepdims=True)
    left_count = jnp.sum(left_mask, axis=1, keepdims=True)
    left_place = window(left_mask, base - left_count + float(KEPT))
    right_place = window(right_mask, base + own_count - float(KEPT))

    def key_segments(mask_place, seg_row):
        return dot_t(jnp.broadcast_to(seg_row, (16, rows_dev)).astype(BF16), mask_place)[0:1]

    key_seg = jnp.concatenate(
        [
            jnp.where(own_mask > 0.5, own_seg, 0.0),
            key_segments(left_place, left_seg),
            key_segments(right_place, right_seg),
        ],
        axis=1,
    )
    nkeys = rows_dev + 2 * WINDOW
    same = iota((rows_dev, rows_dev), 0) == iota((rows_dev, rows_dev), 1)
    seg_diag = jnp.where(same, own_seg, 0.0).astype(BF16)
    mask_diag = jnp.where(same, own_mask, 0.0).astype(BF16)
    query_seg = dot(seg_diag, jnp.ones((rows_dev, nkeys), BF16))
    usable = (query_seg == key_seg) | (
        iota((rows_dev, nkeys), 0) == iota((rows_dev, nkeys), 1)
    )
    usable = jnp.where(usable, 1.0, 0.0)
    usable = jnp.concatenate([usable, usable], axis=0) > 0.5
    kept_column = dot(mask_diag, jnp.ones((rows_dev, width), BF16)) > 0.5
    normed = norm_rows(patches).astype(BF16)

    edge_right.wait_recv()
    edge_left.wait_recv()
    own_rows = xwin[EDGE : EDGE + KEPT].astype(F32)
    kept = jnp.concatenate(
        [
            own_rows[:EDGE]
            + jnp.where(me > 0, lwin[WINDOW - EDGE : WINDOW].astype(F32), 0.0),
            own_rows[EDGE : KEPT - EDGE],
            own_rows[KEPT - EDGE :] + jnp.where(me < ntm - 1, rwin[0:EDGE].astype(F32), 0.0),
        ],
        axis=0,
    )
    for load in loads[3:6]:
        load.wait()
    qkv = dot(norm_rows(kept).astype(BF16), wproj[:, : 3 * half])
    queries = (qkv[:, :half].astype(BF16).astype(F32) * 0.125).astype(BF16)
    kept_kv = qkv[:, half:].astype(BF16)
    npairs = half // 128
    nkv, nq = 4 * nx * KEPT, nz * KEPT
    for p in range(npairs):
        lanes = slice(128 * p, 128 * (p + 1))
        qbuf[p * nq : p * nq + KEPT] = queries[:, lanes]
        kvbuf[p * nkv : p * nkv + KEPT, :128] = kept_kv[:, :half][:, lanes]
        kvbuf[p * nkv : p * nkv + KEPT, 128:] = kept_kv[:, half:][:, lanes]

    def kv_slots(p, first, count):
        return kvbuf.at[p * nkv + first * KEPT : p * nkv + (first + count) * KEPT]

    def q_slot(p, k):
        return qbuf.at[p * nq + k * KEPT : p * nq + (k + 1) * KEPT]

    far_first = sorted(range(1, nz), key=lambda k: -min(k, nz - k))
    far_x = sorted(range(nx), key=lambda k: -min(k, nx - k))
    q_z, kv_x, kv_xy, kv_s = [], [], [], []
    for p in range(npairs):
        q_z.append([])
        kv_x.append([])
        kv_xy.append([])
        own_kv = kv_slots(p, 0, 1)
        for n in range(max(nx, nz)):
            if n < nx:
                k = far_x[n]
                kv_xy[p].append(send(own_kv, kv_slots(p, nx + (nx - k) % nx, 1), xypeer[k]))
            if n < nz - 1:
                k = far_first[n]
                q_z[p].append(send(q_slot(p, 0), q_slot(p, nz - k), zpeer[k]))
            if n < nx - 1:
                k = far_x[n]
                kv_x[p].append(send(own_kv, kv_slots(p, nx - k, 1), xpeer[k]))
        kv_s.append([send(own_kv, kv_slots(p, 2 * nx, 1), sibling)])

    loads[6].wait()
    own_proj = dot(normed, wproj[:, half:])
    keys[0:rows_dev] = own_proj[:, : 2 * half].astype(BF16)
    cross_query = (own_proj[:, 2 * half :].astype(BF16).astype(F32) * 0.125).astype(BF16)

    halo_right.wait_recv()
    halo_left.wait_recv()
    near = jnp.concatenate([lwin[...], rwin[...]], axis=0)
    keys[rows_dev:nkeys] = dot(
        norm_rows(near).astype(BF16), wproj[:, half : 3 * half]
    ).astype(BF16)

    pairs = []

    def cross_pair(i):
        numerator, denominator = attend_pair(
            cross_query[:, 128 * i : 128 * (i + 1)],
            keys[:, 128 * i : 128 * (i + 1)],
            keys[:, half + 128 * i : half + 128 * (i + 1)],
            usable,
        )
        pairs.append((numerator / denominator).astype(BF16))

    for i in range(npairs):
        cross_pair(i)
    loads[7].wait()
    cross_out[...] = dot(jnp.concatenate(pairs, axis=1), wco[...]).astype(BF16)

    half_mod = lax.rem(iota((1, 128), 1), 64)
    block = npairs * KEPT + 16
    head_lane = 64 * lax.rem(iota((16, 128), 0), 2) + 16 * (iota((16, 128), 0) // 2)
    pick = jnp.where(iota((16, 128), 1) == head_lane, 1.0, 0.0)
    pick = jnp.where(iota((16, 128), 0) < 2 * npairs, pick, 0.0).astype(BF16)
    totals, rs_move, packed = [], [], None
    for p in range(npairs):
        for copy in kv_x[p]:
            copy.wait_recv()
        kv_s[p].append(send(kv_slots(p, 1, nx - 1), kv_slots(p, 2 * nx + 1, nx - 1), sibling))
        for copy in kv_xy[p]:
            copy.wait_recv()
        kv_s[p].append(send(kv_slots(p, nx, nx), kv_slots(p, 3 * nx, nx), sibling))
        if p == 0:
            cross_move = send(cross_out, cross_in, partner)
        for copy in q_z[p]:
            copy.wait_recv()
        ring = qbuf[p * nq : (p + 1) * nq]
        first = slice(p * nkv, p * nkv + nkv // 2)
        second = slice(p * nkv + nkv // 2, (p + 1) * nkv)
        num, den = attend_pair(ring, kvbuf[first, :128], kvbuf[first, 128:], None)
        for copy in kv_s[p]:
            copy.wait_recv()
        num2, den2 = attend_pair(ring, kvbuf[second, :128], kvbuf[second, 128:], None)
        num, den = num + num2, den + den2
        packed = den if p == 0 else jnp.where(half_mod >= 16 * p, den, packed)
        totals.append(num[:KEPT])
        num = num.astype(BF16)
        for k in far_first + [0]:
            rows = slice(k * KEPT, (k + 1) * KEPT)
            there = k * block + p * KEPT
            count = KEPT
            if k:
                rsout[there : there + KEPT] = num[rows]
            if p == npairs - 1:
                own = jnp.concatenate([packed[rows], jnp.zeros((128 - KEPT, 128), F32)], axis=0)
                by_head = dot_t(pick, own.astype(BF16))
                count = KEPT + 16
                if k:
                    rsout[there + KEPT : there + count] = by_head.astype(BF16)
                else:
                    totals.append(by_head)
            if k:
                back = (nz - k) * block + p * KEPT
                rs_move.append(
                    send(rsout.at[there : there + count], rsin.at[back : back + count], zpeer[k])
                )

    for copy in rs_move:
        copy.wait_recv()
    for p in range(npairs + 1):
        for k in range(1, nz):
            there = k * block + p * KEPT
            totals[p] += rsin[there : there + totals[p].shape[0]].astype(F32)
    by_head = totals[npairs]
    inverse = jnp.where(by_head > 0.0, 1.0 / by_head, 0.0)
    coarse = inverse.astype(BF16)
    fine = (inverse - coarse.astype(F32)).astype(BF16)
    widen = jnp.where(iota((16, half), 1) // 64 == iota((16, half), 0), 1.0, 0.0).astype(BF16)
    inverse = (dot_0(coarse, widen) + dot_0(fine, widen))[:KEPT]
    attention = [
        (totals[p] * inverse[:, 128 * p : 128 * (p + 1)]).astype(BF16) for p in range(npairs)
    ]
    loads[8].wait()
    attn_out[...] = dot(jnp.concatenate(attention, axis=1), wo[...]).astype(BF16)
    attn_move = send(attn_out, attn_in, partner)
    loads[9].wait()
    loads[10].wait()
    attn_move.wait_recv()
    hidden = kept + (attn_out[...].astype(F32) + attn_in[...].astype(F32))
    edge_hidden[0:EDGE] = hidden[:EDGE]
    edge_hidden[EDGE : 2 * EDGE] = hidden[KEPT - EDGE :]
    hidden_right = send(edge_hidden.at[EDGE : 2 * EDGE], left_hidden, right_side)
    hidden_left = send(edge_hidden.at[0:EDGE], right_hidden, left_side)
    gated = jax.nn.gelu(dot(norm_rows(hidden).astype(BF16), wu[...]), approximate=True)
    down_out[...] = dot(gated.astype(BF16), wd[...]).astype(BF16)
    ends = []
    for n, side in enumerate((mp, 1 - mp)):
        there = slice(n * EDGE, (n + 1) * EDGE)
        ends.append(send(down_out.at[KEPT - EDGE : KEPT], left_down.at[there], (right, side)))
        ends.append(send(down_out.at[0:EDGE], right_down.at[there], (left, side)))
    down_move = send(down_out, down_in, partner)
    hidden_right.wait_recv()
    hidden_left.wait_recv()
    down_move.wait_recv()
    own_result = hidden + (down_out[...].astype(F32) + down_in[...].astype(F32))
    for copy in ends:
        copy.wait_recv()

    def edge_result(base_ref, parts_ref):
        parts = parts_ref[...].astype(F32)
        return base_ref[...] + (parts[:EDGE] + parts[EDGE:])

    cross_move.wait_recv()
    pruned = patches.astype(F32) + (cross_out[...].astype(F32) + cross_in[...].astype(F32))

    finished = jnp.concatenate(
        [
            edge_result(left_hidden, left_down),
            own_result,
            edge_result(right_hidden, right_down),
        ],
        axis=0,
    )
    spread = dot_0(own_place, finished.astype(BF16))
    out_ref[...] = jnp.where(kept_column, spread, pruned).astype(BF16)

    for copy in started:
        copy.wait_send()


def body(nx, nz, patches, keep_mask, segment, *weights):
    rows, width = patches.shape
    half = weights[0].shape[1]
    hidden = weights[6].shape[1]
    ntm = nx * nz * 4
    npairs = half // 128
    copies = 14 + npairs * (2 * nx + 2 + 2 * (nz - 1))
    vmem = lambda *shape: pltpu.VMEM(shape, BF16)
    return pl.pallas_call(
        functools.partial(kernel, nx, nz),
        out_shape=pltpu.VMEM((rows, width), BF16),
        in_specs=[pl.BlockSpec(memory_space=pl.ANY)] * 11,
        out_specs=pl.BlockSpec(memory_space=pltpu.VMEM),
        scratch_shapes=[
            vmem(rows, width),
            pltpu.VMEM((ntm * rows // 128, 128), jnp.int32),
            pltpu.VMEM((ntm * rows // 128, 128), jnp.int32),
            vmem(width, 4 * half),
            vmem(half, width),
            vmem(half, width),
            vmem(width, hidden),
            vmem(hidden, width),
            vmem(WINDOW, width),
            vmem(WINDOW, width),
            vmem(WINDOW, width),
            vmem(npairs * 4 * nx * KEPT, 256),
            vmem(npairs * nz * KEPT, 128),
            vmem(nz * (npairs * KEPT + 16), 128),
            vmem(nz * (npairs * KEPT + 16), 128),
            vmem(rows + 2 * WINDOW, 2 * half),
            vmem(KEPT, width),
            vmem(KEPT, width),
            vmem(rows, width),
            vmem(rows, width),
            vmem(KEPT, width),
            vmem(KEPT, width),
            pltpu.VMEM((2 * EDGE, width), F32),
            pltpu.VMEM((EDGE, width), F32),
            pltpu.VMEM((EDGE, width), F32),
            vmem(2 * EDGE, width),
            vmem(2 * EDGE, width),
            pltpu.SemaphoreType.DMA((11,)),
            pltpu.SemaphoreType.DMA((copies,)),
            pltpu.SemaphoreType.DMA((copies,)),
        ],
        compiler_params=pltpu.CompilerParams(
            collective_id=0, has_side_effects=True, vmem_limit_bytes=60 * 1024 * 1024
        ),
    )(patches, keep_mask.reshape(-1, 128), segment.reshape(-1, 128), *weights)


def solution(mesh):
    placed = (
        P("tm", None),
        P(),
        P(),
        P(None, "mp"),
        P(None, "mp"),
        P(None, "mp"),
        P("mp", None),
        P(None, "mp"),
        P("mp", None),
        P(None, "mp"),
        P("mp", None),
    )
    ntm = mesh.shape["tm"]
    nx = 4 if ntm == 128 else 2
    return jax.shard_map(
        functools.partial(body, nx, ntm // (4 * nx)),
        mesh=mesh,
        in_specs=placed,
        out_specs=P("tm", None),
        check_vma=False,
    )
```

```python
import functools

import jax
import jax.numpy as jnp
from jax import lax
from jax.experimental import pallas as pl
from jax.experimental.pallas import tpu as pltpu
from jax.sharding import PartitionSpec as P

KEPT = 48
EDGE = 16
WINDOW = KEPT + 2 * EDGE
F32 = jnp.float32
BF16 = jnp.bfloat16


def norm_rows(values):
    values = values.astype(F32)
    center = values - jnp.mean(values, axis=-1, keepdims=True)
    return center * lax.rsqrt(jnp.mean(center * center, axis=-1, keepdims=True) + 1e-05)


def dot(a, b):
    return jnp.dot(a, b, preferred_element_type=F32)


def dot_t(a, b):
    return lax.dot_general(a, b, (((1,), (1,)), ((), ())), preferred_element_type=F32)


def dot_0(a, b):
    return lax.dot_general(a, b, (((0,), (0,)), ((), ())), preferred_element_type=F32)


def iota(shape, dim):
    return lax.broadcasted_iota(jnp.int32, shape, dim)


def attend_pair(queries, keys, values, usable):
    rows = queries.shape[0]
    low = iota((rows, 128), 1) < 64
    zero = jnp.zeros_like(queries)
    both = jnp.concatenate([jnp.where(low, queries, zero), jnp.where(low, zero, queries)], axis=0)
    weight = jnp.exp(dot_t(both, keys))
    if usable is not None:
        weight = jnp.where(usable, weight, 0.0)
    ones = jnp.ones((keys.shape[0], 128), BF16)
    total = dot(weight.astype(BF16), jnp.concatenate([values, ones], axis=1))
    numerator = jnp.where(low, total[:rows, :128], total[rows:, :128])
    denominator = jnp.where(low, total[:rows, 128:], total[rows:, 128:])
    return numerator, denominator


class Move:
    def __init__(self, copy, going, coming):
        self.copy, self.going, self.coming = copy, going, coming

    def start(self):
        self.run(self.going, self.copy.start)

    def wait_recv(self):
        self.run(self.coming, self.copy.wait_recv)

    def wait_send(self):
        self.run(self.going, self.copy.wait_send)

    def run(self, condition, step):
        if condition is None:
            step()
        else:
            pl.when(condition)(lambda: step())


def kernel(
    nx,
    nz,
    patches_hbm,
    mask_hbm,
    seg_hbm,
    wq_hbm,
    wk_hbm,
    wv_hbm,
    wo_hbm,
    wcq_hbm,
    wco_hbm,
    wu_hbm,
    wd_hbm,
    out_ref,
    patches_ref,
    mask_ref,
    seg_ref,
    wproj,
    wo,
    wco,
    wu,
    wd,
    xwin,
    lwin,
    rwin,
    kvbuf,
    qbuf,
    rsout,
    rsin,
    keys,
    attn_out,
    attn_in,
    cross_out,
    cross_in,
    down_out,
    down_in,
    edge_hidden,
    left_hidden,
    right_hidden,
    left_down,
    right_down,
    wsem,
    ssem,
    rsem,
):
    ntm = nx * nz * 4
    rows_dev, width = patches_hbm.shape
    half = wq_hbm.shape[1]
    me = lax.axis_index("tm")
    mp = lax.axis_index("mp")
    core = lax.rem(me, 2)
    yh = lax.rem(me // 2, 2)
    z = lax.rem(me // 4, nz)
    x = me // (4 * nz)
    sibling = (me + 1 - 2 * core, mp)
    ypart = me + 2 - 4 * yh
    right = lax.rem(me + 1, ntm)
    left = lax.rem(me + ntm - 1, ntm)
    right_side = (right, mp + core * (1 - 2 * mp))
    left_side = (left, mp + (1 - core) * (1 - 2 * mp))
    partner = (me, 1 - mp)
    zpeer = [(me + 4 * (lax.rem(z + k, nz) - z), mp) for k in range(nz)]
    xpeer = [(me + 4 * nz * (lax.rem(x + k, nx) - x), mp) for k in range(nx)]
    xypeer = [(ypart + 4 * nz * (lax.rem(x + k, nx) - x), mp) for k in range(nx)]
    has_left, has_right = me > 0, me < ntm - 1

    barrier = pltpu.get_barrier_semaphore()

    def greet(targets):
        for target in targets:
            pl.semaphore_signal(
                barrier, inc=1, device_id=target, device_id_type=pl.DeviceIdType.MESH
            )

    fixed = [sibling, partner] + zpeer[1:] + xpeer[1:] + xypeer
    greet(fixed)
    pl.when(has_left)(lambda: greet([(left, mp), (left, 1 - mp)]))
    pl.when(has_right)(lambda: greet([(right, mp), (right, 1 - mp)]))
    greeted = len(fixed) + 2 * jnp.minimum(me, 1) + 2 * jnp.minimum(ntm - 1 - me, 1)

    sources = [
        (mask_hbm, mask_ref),
        (patches_hbm, patches_ref),
        (seg_hbm, seg_ref),
        (wq_hbm, wproj.at[:, 0:half]),
        (wk_hbm, wproj.at[:, half : 2 * half]),
        (wv_hbm, wproj.at[:, 2 * half : 3 * half]),
        (wcq_hbm, wproj.at[:, 3 * half : 4 * half]),
        (wco_hbm, wco),
        (wo_hbm, wo),
        (wu_hbm, wu),
        (wd_hbm, wd),
    ]
    loads = []
    for i, (source, target) in enumerate(sources):
        load = pltpu.make_async_copy(source, target, wsem.at[i])
        load.start()
        loads.append(load)

    counter = [0]
    started = []

    def send(source, target, where, going=None, coming=None):
        i = counter[0]
        counter[0] += 1
        copy = pltpu.make_async_remote_copy(
            src_ref=source,
            dst_ref=target,
            send_sem=ssem.at[i],
            recv_sem=rsem.at[i],
            device_id=where,
            device_id_type=pl.DeviceIdType.MESH,
        )
        move = Move(copy, going, coming)
        move.start()
        started.append(move)
        return move

    def send_right(source, target, where):
        return send(source, target, where, has_right, has_left)

    def send_left(source, target, where):
        return send(source, target, where, has_left, has_right)

    loads[0].wait()
    mask = mask_ref[...].astype(F32)
    place = iota(mask.shape, 0) * 128 + iota(mask.shape, 1)
    before = jnp.where(place < me * rows_dev, mask, 0.0)
    base = jnp.sum(jnp.sum(before, axis=1, keepdims=True), axis=0, keepdims=True)
    base = base - (KEPT * me).astype(F32)

    def run_of(ref, index):
        first = index * rows_dev // 128
        both = jnp.concatenate([ref[pl.ds(first, 1), :], ref[pl.ds(first + 1, 1), :]], axis=1)
        phase = lax.rem(index, 4)
        row = both[:, 0:rows_dev]
        for k in range(1, 4):
            row = jnp.where(phase == k, both[:, 32 * k : 32 * k + rows_dev], row)
        return row.astype(F32)

    own_mask = run_of(mask_ref, me)
    left_mask = jnp.where(me > 0, run_of(mask_ref, left), 0.0)
    right_mask = jnp.where(me < ntm - 1, run_of(mask_ref, right), 0.0)
    earlier = (iota((rows_dev, rows_dev), 0) < iota((rows_dev, rows_dev), 1)).astype(F32)
    earlier = earlier.astype(BF16)

    def window(mask_row, base_row):
        rank = dot(jnp.broadcast_to(mask_row, (16, rows_dev)).astype(BF16), earlier)[0:1]
        slot = jnp.where(mask_row > 0.5, rank + base_row + float(EDGE), -1.0)
        grid = iota((WINDOW, rows_dev), 0).astype(F32)
        return jnp.where(grid == slot, 1.0, 0.0).astype(BF16)

    own_place = window(own_mask, base)
    loads[1].wait()
    patches = patches_ref[...]
    xwin[...] = dot(own_place, patches).astype(BF16)

    def clear(*refs):
        for ref in refs:
            ref[...] = jnp.zeros(ref.shape, ref.dtype)

    pl.when(me == 0)(lambda: clear(lwin, left_hidden, left_down))
    pl.when(me == ntm - 1)(lambda: clear(rwin, right_hidden, right_down))

    pl.semaphore_wait(barrier, greeted)

    edge_right = send_right(xwin.at[KEPT + EDGE : WINDOW], lwin.at[KEPT + EDGE : WINDOW], right_side)
    edge_left = send_left(xwin.at[0:EDGE], rwin.at[0:EDGE], left_side)
    halo_right = send_right(xwin.at[0 : KEPT + EDGE], lwin.at[0 : KEPT + EDGE], right_side)
    halo_left = send_left(xwin.at[EDGE:WINDOW], rwin.at[EDGE:WINDOW], left_side)

    loads[2].wait()
    own_seg = run_of(seg_ref, me) + 1.0
    left_seg = run_of(seg_ref, left) + 1.0
    right_seg = run_of(seg_ref, right) + 1.0
    own_count = jnp.sum(own_mask, axis=1, keepdims=True)
    left_count = jnp.sum(left_mask, axis=1, keepdims=True)
    left_place = window(left_mask, base - left_count + float(KEPT))
    right_place = window(right_mask, base + own_count - float(KEPT))

    def key_segments(mask_place, seg_row):
        return dot_t(jnp.broadcast_to(seg_row, (16, rows_dev)).astype(BF16), mask_place)[0:1]

    key_seg = jnp.concatenate(
        [
            jnp.where(own_mask > 0.5, own_seg, 0.0),
            key_segments(left_place, left_seg),
            key_segments(right_place, right_seg),
        ],
        axis=1,
    )
    nkeys = rows_dev + 2 * WINDOW
    same = iota((rows_dev, rows_dev), 0) == iota((rows_dev, rows_dev), 1)
    seg_diag = jnp.where(same, own_seg, 0.0).astype(BF16)
    mask_diag = jnp.where(same, own_mask, 0.0).astype(BF16)
    query_seg = dot(seg_diag, jnp.ones((rows_dev, nkeys), BF16))
    usable = (query_seg == key_seg) | (
        iota((rows_dev, nkeys), 0) == iota((rows_dev, nkeys), 1)
    )
    usable = jnp.where(usable, 1.0, 0.0)
    usable = jnp.concatenate([usable, usable], axis=0) > 0.5
    kept_column = dot(mask_diag, jnp.ones((rows_dev, width), BF16)) > 0.5
    normed = norm_rows(patches).astype(BF16)

    edge_right.wait_recv()
    edge_left.wait_recv()
    own_rows = xwin[EDGE : EDGE + KEPT].astype(F32)
    kept = jnp.concatenate(
        [
            own_rows[:EDGE]
            + lwin[WINDOW - EDGE : WINDOW].astype(F32),
            own_rows[EDGE : KEPT - EDGE],
            own_rows[KEPT - EDGE :] + rwin[0:EDGE].astype(F32),
        ],
        axis=0,
    )
    for load in loads[3:6]:
        load.wait()
    qkv = dot(norm_rows(kept).astype(BF16), wproj[:, : 3 * half])
    queries = (qkv[:, :half].astype(BF16).astype(F32) * 0.125).astype(BF16)
    kept_kv = qkv[:, half:].astype(BF16)
    npairs = half // 128
    nkv, nq = 4 * nx * KEPT, nz * KEPT
    for p in range(npairs):
        lanes = slice(128 * p, 128 * (p + 1))
        qbuf[p * nq : p * nq + KEPT] = queries[:, lanes]
        kvbuf[p * nkv : p * nkv + KEPT, :128] = kept_kv[:, :half][:, lanes]
        kvbuf[p * nkv : p * nkv + KEPT, 128:] = kept_kv[:, half:][:, lanes]

    def kv_slots(p, first, count):
        return kvbuf.at[p * nkv + first * KEPT : p * nkv + (first + count) * KEPT]

    def q_slot(p, k):
        return qbuf.at[p * nq + k * KEPT : p * nq + (k + 1) * KEPT]

    far_first = sorted(range(1, nz), key=lambda k: -min(k, nz - k))
    far_x = sorted(range(nx), key=lambda k: -min(k, nx - k))
    q_z, kv_x, kv_xy, kv_s = [], [], [], []
    for p in range(npairs):
        q_z.append([])
        kv_x.append([])
        kv_xy.append([])
        own_kv = kv_slots(p, 0, 1)
        for n in range(max(nx, nz)):
            if n < nx:
                k = far_x[n]
                kv_xy[p].append(send(own_kv, kv_slots(p, nx + (nx - k) % nx, 1), xypeer[k]))
            if n < nz - 1:
                k = far_first[n]
                q_z[p].append(send(q_slot(p, 0), q_slot(p, nz - k), zpeer[k]))
            if n < nx - 1:
                k = far_x[n]
                kv_x[p].append(send(own_kv, kv_slots(p, nx - k, 1), xpeer[k]))
        kv_s.append([send(own_kv, kv_slots(p, 2 * nx, 1), sibling)])

    loads[6].wait()
    own_proj = dot(normed, wproj[:, half:])
    keys[0:rows_dev] = own_proj[:, : 2 * half].astype(BF16)
    cross_query = (own_proj[:, 2 * half :].astype(BF16).astype(F32) * 0.125).astype(BF16)

    halo_right.wait_recv()
    halo_left.wait_recv()
    near = jnp.concatenate([lwin[...], rwin[...]], axis=0)
    keys[rows_dev:nkeys] = dot(
        norm_rows(near).astype(BF16), wproj[:, half : 3 * half]
    ).astype(BF16)

    pairs = []

    def cross_pair(i):
        numerator, denominator = attend_pair(
            cross_query[:, 128 * i : 128 * (i + 1)],
            keys[:, 128 * i : 128 * (i + 1)],
            keys[:, half + 128 * i : half + 128 * (i + 1)],
            usable,
        )
        pairs.append((numerator / denominator).astype(BF16))

    for i in range(npairs):
        cross_pair(i)
    loads[7].wait()
    cross_out[...] = dot(jnp.concatenate(pairs, axis=1), wco[...]).astype(BF16)

    half_mod = lax.rem(iota((1, 128), 1), 64)
    block = npairs * KEPT + 16
    head_lane = 64 * lax.rem(iota((16, 128), 0), 2) + 16 * (iota((16, 128), 0) // 2)
    pick = jnp.where(iota((16, 128), 1) == head_lane, 1.0, 0.0)
    pick = jnp.where(iota((16, 128), 0) < 2 * npairs, pick, 0.0).astype(BF16)
    totals, rs_move, packed = [], [], None
    for p in range(npairs):
        for copy in kv_x[p]:
            copy.wait_recv()
        kv_s[p].append(send(kv_slots(p, 1, nx - 1), kv_slots(p, 2 * nx + 1, nx - 1), sibling))
        for copy in kv_xy[p]:
            copy.wait_recv()
        kv_s[p].append(send(kv_slots(p, nx, nx), kv_slots(p, 3 * nx, nx), sibling))
        if p == 0:
            cross_move = send(cross_out, cross_in, partner)
        for copy in q_z[p]:
            copy.wait_recv()
        ring = qbuf[p * nq : (p + 1) * nq]
        first = slice(p * nkv, p * nkv + nkv // 2)
        second = slice(p * nkv + nkv // 2, (p + 1) * nkv)
        num, den = attend_pair(ring, kvbuf[first, :128], kvbuf[first, 128:], None)
        for copy in kv_s[p]:
            copy.wait_recv()
        num2, den2 = attend_pair(ring, kvbuf[second, :128], kvbuf[second, 128:], None)
        num, den = num + num2, den + den2
        packed = den if p == 0 else jnp.where(half_mod >= 16 * p, den, packed)
        totals.append(num[:KEPT])
        num = num.astype(BF16)
        for k in far_first + [0]:
            rows = slice(k * KEPT, (k + 1) * KEPT)
            there = k * block + p * KEPT
            count = KEPT
            if k:
                rsout[there : there + KEPT] = num[rows]
            if p == npairs - 1:
                own = jnp.concatenate([packed[rows], jnp.zeros((128 - KEPT, 128), F32)], axis=0)
                by_head = dot_t(pick, own.astype(BF16))
                count = KEPT + 16
                if k:
                    rsout[there + KEPT : there + count] = by_head.astype(BF16)
                else:
                    totals.append(by_head)
            if k:
                back = (nz - k) * block + p * KEPT
                rs_move.append(
                    send(rsout.at[there : there + count], rsin.at[back : back + count], zpeer[k])
                )

    for p in range(npairs + 1):
        for copy in rs_move[p * (nz - 1) : (p + 1) * (nz - 1)]:
            copy.wait_recv()
        for k in range(1, nz):
            there = k * block + p * KEPT
            totals[p] += rsin[there : there + totals[p].shape[0]].astype(F32)
    by_head = totals[npairs]
    inverse = jnp.where(by_head > 0.0, 1.0 / by_head, 0.0)
    coarse = inverse.astype(BF16)
    fine = (inverse - coarse.astype(F32)).astype(BF16)
    widen = jnp.where(iota((16, half), 1) // 64 == iota((16, half), 0), 1.0, 0.0).astype(BF16)
    inverse = (dot_0(coarse, widen) + dot_0(fine, widen))[:KEPT]
    attention = [
        (totals[p] * inverse[:, 128 * p : 128 * (p + 1)]).astype(BF16) for p in range(npairs)
    ]
    loads[8].wait()
    attn_out[...] = dot(jnp.concatenate(attention, axis=1), wo[...]).astype(BF16)
    attn_move = send(attn_out, attn_in, partner)
    loads[9].wait()
    loads[10].wait()
    attn_move.wait_recv()
    hidden = kept + (attn_out[...].astype(F32) + attn_in[...].astype(F32))
    edge_hidden[0:EDGE] = hidden[:EDGE]
    edge_hidden[EDGE : 2 * EDGE] = hidden[KEPT - EDGE :]
    hidden_right = send_right(edge_hidden.at[EDGE : 2 * EDGE], left_hidden, right_side)
    hidden_left = send_left(edge_hidden.at[0:EDGE], right_hidden, left_side)
    gated = jax.nn.gelu(dot(norm_rows(hidden).astype(BF16), wu[...]), approximate=True)
    down_out[...] = dot(gated.astype(BF16), wd[...]).astype(BF16)
    ends = []
    for n, side in enumerate((mp, 1 - mp)):
        there = slice(n * EDGE, (n + 1) * EDGE)
        ends.append(send_right(down_out.at[KEPT - EDGE : KEPT], left_down.at[there], (right, side)))
        ends.append(send_left(down_out.at[0:EDGE], right_down.at[there], (left, side)))
    down_move = send(down_out, down_in, partner)
    hidden_right.wait_recv()
    hidden_left.wait_recv()
    down_move.wait_recv()
    own_result = hidden + (down_out[...].astype(F32) + down_in[...].astype(F32))
    for copy in ends:
        copy.wait_recv()

    def edge_result(base_ref, parts_ref):
        parts = parts_ref[...].astype(F32)
        return base_ref[...] + (parts[:EDGE] + parts[EDGE:])

    cross_move.wait_recv()
    pruned = patches.astype(F32) + (cross_out[...].astype(F32) + cross_in[...].astype(F32))

    finished = jnp.concatenate(
        [
            edge_result(left_hidden, left_down),
            own_result,
            edge_result(right_hidden, right_down),
        ],
        axis=0,
    )
    spread = dot_0(own_place, finished.astype(BF16))
    out_ref[...] = jnp.where(kept_column, spread, pruned).astype(BF16)

    for copy in started:
        copy.wait_send()


def body(nx, nz, patches, keep_mask, segment, *weights):
    rows, width = patches.shape
    half = weights[0].shape[1]
    hidden = weights[6].shape[1]
    ntm = nx * nz * 4
    npairs = half // 128
    copies = 14 + npairs * (2 * nx + 2 + 2 * (nz - 1))
    vmem = lambda *shape: pltpu.VMEM(shape, BF16)
    return pl.pallas_call(
        functools.partial(kernel, nx, nz),
        out_shape=pltpu.VMEM((rows, width), BF16),
        in_specs=[pl.BlockSpec(memory_space=pl.ANY)] * 11,
        out_specs=pl.BlockSpec(memory_space=pltpu.VMEM),
        scratch_shapes=[
            vmem(rows, width),
            pltpu.VMEM((ntm * rows // 128, 128), jnp.int32),
            pltpu.VMEM((ntm * rows // 128, 128), jnp.int32),
            vmem(width, 4 * half),
            vmem(half, width),
            vmem(half, width),
            vmem(width, hidden),
            vmem(hidden, width),
            vmem(WINDOW, width),
            vmem(WINDOW, width),
            vmem(WINDOW, width),
            vmem(npairs * 4 * nx * KEPT, 256),
            vmem(npairs * nz * KEPT, 128),
            vmem(nz * (npairs * KEPT + 16), 128),
            vmem(nz * (npairs * KEPT + 16), 128),
            vmem(rows + 2 * WINDOW, 2 * half),
            vmem(KEPT, width),
            vmem(KEPT, width),
            vmem(rows, width),
            vmem(rows, width),
            vmem(KEPT, width),
            vmem(KEPT, width),
            pltpu.VMEM((2 * EDGE, width), F32),
            pltpu.VMEM((EDGE, width), F32),
            pltpu.VMEM((EDGE, width), F32),
            vmem(2 * EDGE, width),
            vmem(2 * EDGE, width),
            pltpu.SemaphoreType.DMA((11,)),
            pltpu.SemaphoreType.DMA((copies,)),
            pltpu.SemaphoreType.DMA((copies,)),
        ],
        compiler_params=pltpu.CompilerParams(
            collective_id=0, has_side_effects=True, vmem_limit_bytes=60 * 1024 * 1024
        ),
    )(patches, keep_mask.reshape(-1, 128), segment.reshape(-1, 128), *weights)


def solution(mesh):
    placed = (
        P("tm", None),
        P(),
        P(),
        P(None, "mp"),
        P(None, "mp"),
        P(None, "mp"),
        P("mp", None),
        P(None, "mp"),
        P("mp", None),
        P(None, "mp"),
        P("mp", None),
    )
    ntm = mesh.shape["tm"]
    nx = 4 if ntm == 128 else 2
    return jax.shard_map(
        functools.partial(body, nx, ntm // (4 * nx)),
        mesh=mesh,
        in_specs=placed,
        out_specs=P("tm", None),
        check_vma=False,
    )
```

```python
import functools

import jax
import jax.numpy as jnp
from jax import lax
from jax.experimental import pallas as pl
from jax.experimental.pallas import tpu as pltpu
from jax.sharding import PartitionSpec as P

KEPT = 48
EDGE = 16
WINDOW = KEPT + 2 * EDGE
F32 = jnp.float32
BF16 = jnp.bfloat16


def norm_rows(values):
    values = values.astype(F32)
    center = values - jnp.mean(values, axis=-1, keepdims=True)
    return center * lax.rsqrt(jnp.mean(center * center, axis=-1, keepdims=True) + 1e-05)


def dot(a, b):
    return jnp.dot(a, b, preferred_element_type=F32)


def dot_t(a, b):
    return lax.dot_general(a, b, (((1,), (1,)), ((), ())), preferred_element_type=F32)


def dot_0(a, b):
    return lax.dot_general(a, b, (((0,), (0,)), ((), ())), preferred_element_type=F32)


def iota(shape, dim):
    return lax.broadcasted_iota(jnp.int32, shape, dim)


def attend_pair(queries, keys, values, usable):
    rows = queries.shape[0]
    low = iota((rows, 128), 1) < 64
    zero = jnp.zeros_like(queries)
    both = jnp.concatenate([jnp.where(low, queries, zero), jnp.where(low, zero, queries)], axis=0)
    weight = jnp.exp(dot_t(both, keys))
    if usable is not None:
        weight = jnp.where(usable, weight, 0.0)
    ones = jnp.ones((keys.shape[0], 128), BF16)
    total = dot(weight.astype(BF16), jnp.concatenate([values, ones], axis=1))
    numerator = jnp.where(low, total[:rows, :128], total[rows:, :128])
    denominator = jnp.where(low, total[:rows, 128:], total[rows:, 128:])
    return numerator, denominator


class Move:
    def __init__(self, copy, going, coming):
        self.copy, self.going, self.coming = copy, going, coming

    def start(self):
        self.run(self.going, self.copy.start)

    def wait_recv(self):
        self.run(self.coming, self.copy.wait_recv)

    def wait_send(self):
        self.run(self.going, self.copy.wait_send)

    def run(self, condition, step):
        if condition is None:
            step()
        else:
            pl.when(condition)(lambda: step())


def kernel(
    nx,
    nz,
    patches_hbm,
    mask_hbm,
    seg_hbm,
    wq_hbm,
    wk_hbm,
    wv_hbm,
    wo_hbm,
    wcq_hbm,
    wco_hbm,
    wu_hbm,
    wd_hbm,
    out_ref,
    patches_ref,
    mask_ref,
    seg_ref,
    wproj,
    wo,
    wco,
    wu,
    wd,
    xwin,
    lwin,
    rwin,
    kvbuf,
    qbuf,
    rsout,
    rsin,
    keys,
    attn_out,
    attn_in,
    cross_out,
    cross_in,
    down_out,
    down_in,
    edge_hidden,
    left_hidden,
    right_hidden,
    left_down,
    right_down,
    wsem,
    ssem,
    rsem,
):
    ntm = nx * nz * 4
    rows_dev, width = patches_hbm.shape
    half = wq_hbm.shape[1]
    me = lax.axis_index("tm")
    mp = lax.axis_index("mp")
    core = lax.rem(me, 2)
    yh = lax.rem(me // 2, 2)
    z = lax.rem(me // 4, nz)
    x = me // (4 * nz)
    sibling = (me + 1 - 2 * core, mp)
    ypart = me + 2 - 4 * yh
    right = lax.rem(me + 1, ntm)
    left = lax.rem(me + ntm - 1, ntm)
    right_side = (right, mp + core * (1 - 2 * mp))
    left_side = (left, mp + (1 - core) * (1 - 2 * mp))
    partner = (me, 1 - mp)
    zpeer = [(me + 4 * (lax.rem(z + k, nz) - z), mp) for k in range(nz)]
    xpeer = [(me + 4 * nz * (lax.rem(x + k, nx) - x), mp) for k in range(nx)]
    xypeer = [(ypart + 4 * nz * (lax.rem(x + k, nx) - x), mp) for k in range(nx)]
    has_left, has_right = me > 0, me < ntm - 1

    barrier = pltpu.get_barrier_semaphore()

    def greet(targets):
        for target in targets:
            pl.semaphore_signal(
                barrier, inc=1, device_id=target, device_id_type=pl.DeviceIdType.MESH
            )

    fixed = [sibling, partner] + zpeer[1:] + xpeer[1:] + xypeer
    greet(fixed)
    pl.when(has_left)(lambda: greet([(left, mp), (left, 1 - mp)]))
    pl.when(has_right)(lambda: greet([(right, mp), (right, 1 - mp)]))
    greeted = len(fixed) + 2 * jnp.minimum(me, 1) + 2 * jnp.minimum(ntm - 1 - me, 1)

    sources = [
        (mask_hbm, mask_ref),
        (patches_hbm, patches_ref),
        (seg_hbm, seg_ref),
    ]
    npairs = half // 128
    for p in range(npairs):
        for n, weight in enumerate((wq_hbm, wk_hbm, wv_hbm)):
            there = (3 * p + n) * 128
            sources.append(
                (weight.at[:, 128 * p : 128 * (p + 1)], wproj.at[:, there : there + 128])
            )
    sources += [
        (wcq_hbm, wproj.at[:, 3 * half : 4 * half]),
        (wco_hbm, wco),
        (wo_hbm, wo),
        (wu_hbm, wu),
        (wd_hbm, wd),
    ]
    loads = []
    for i, (source, target) in enumerate(sources):
        load = pltpu.make_async_copy(source, target, wsem.at[i])
        load.start()
        loads.append(load)

    pair_loads = loads[3 : 3 + 3 * npairs]
    loads = loads[:3] + [None] * 3 + loads[3 + 3 * npairs :]

    counter = [0]
    started = []

    def send(source, target, where, going=None, coming=None):
        i = counter[0]
        counter[0] += 1
        copy = pltpu.make_async_remote_copy(
            src_ref=source,
            dst_ref=target,
            send_sem=ssem.at[i],
            recv_sem=rsem.at[i],
            device_id=where,
            device_id_type=pl.DeviceIdType.MESH,
        )
        move = Move(copy, going, coming)
        move.start()
        started.append(move)
        return move

    def send_right(source, target, where):
        return send(source, target, where, has_right, has_left)

    def send_left(source, target, where):
        return send(source, target, where, has_left, has_right)

    loads[0].wait()
    mask = mask_ref[...].astype(F32)
    place = iota(mask.shape, 0) * 128 + iota(mask.shape, 1)
    before = jnp.where(place < me * rows_dev, mask, 0.0)
    base = jnp.sum(jnp.sum(before, axis=1, keepdims=True), axis=0, keepdims=True)
    base = base - (KEPT * me).astype(F32)

    def run_of(ref, index):
        first = index * rows_dev // 128
        both = jnp.concatenate([ref[pl.ds(first, 1), :], ref[pl.ds(first + 1, 1), :]], axis=1)
        phase = lax.rem(index, 4)
        row = both[:, 0:rows_dev]
        for k in range(1, 4):
            row = jnp.where(phase == k, both[:, 32 * k : 32 * k + rows_dev], row)
        return row.astype(F32)

    own_mask = run_of(mask_ref, me)
    left_mask = jnp.where(me > 0, run_of(mask_ref, left), 0.0)
    right_mask = jnp.where(me < ntm - 1, run_of(mask_ref, right), 0.0)
    earlier = (iota((rows_dev, rows_dev), 0) < iota((rows_dev, rows_dev), 1)).astype(F32)
    earlier = earlier.astype(BF16)

    def window(mask_row, base_row):
        rank = dot(jnp.broadcast_to(mask_row, (16, rows_dev)).astype(BF16), earlier)[0:1]
        slot = jnp.where(mask_row > 0.5, rank + base_row + float(EDGE), -1.0)
        grid = iota((WINDOW, rows_dev), 0).astype(F32)
        return jnp.where(grid == slot, 1.0, 0.0).astype(BF16)

    own_place = window(own_mask, base)
    loads[1].wait()
    patches = patches_ref[...]
    xwin[...] = dot(own_place, patches).astype(BF16)

    def clear(*refs):
        for ref in refs:
            ref[...] = jnp.zeros(ref.shape, ref.dtype)

    pl.when(me == 0)(lambda: clear(lwin, left_hidden, left_down))
    pl.when(me == ntm - 1)(lambda: clear(rwin, right_hidden, right_down))

    pl.semaphore_wait(barrier, greeted)

    edge_right = send_right(xwin.at[KEPT + EDGE : WINDOW], lwin.at[KEPT + EDGE : WINDOW], right_side)
    edge_left = send_left(xwin.at[0:EDGE], rwin.at[0:EDGE], left_side)
    halo_right = send_right(xwin.at[0 : KEPT + EDGE], lwin.at[0 : KEPT + EDGE], right_side)
    halo_left = send_left(xwin.at[EDGE:WINDOW], rwin.at[EDGE:WINDOW], left_side)

    loads[2].wait()
    own_seg = run_of(seg_ref, me) + 1.0
    left_seg = run_of(seg_ref, left) + 1.0
    right_seg = run_of(seg_ref, right) + 1.0
    own_count = jnp.sum(own_mask, axis=1, keepdims=True)
    left_count = jnp.sum(left_mask, axis=1, keepdims=True)
    left_place = window(left_mask, base - left_count + float(KEPT))
    right_place = window(right_mask, base + own_count - float(KEPT))

    def key_segments(mask_place, seg_row):
        return dot_t(jnp.broadcast_to(seg_row, (16, rows_dev)).astype(BF16), mask_place)[0:1]

    key_seg = jnp.concatenate(
        [
            jnp.where(own_mask > 0.5, own_seg, 0.0),
            key_segments(left_place, left_seg),
            key_segments(right_place, right_seg),
        ],
        axis=1,
    )
    nkeys = rows_dev + 2 * WINDOW
    same = iota((rows_dev, rows_dev), 0) == iota((rows_dev, rows_dev), 1)
    seg_diag = jnp.where(same, own_seg, 0.0).astype(BF16)
    mask_diag = jnp.where(same, own_mask, 0.0).astype(BF16)
    query_seg = dot(seg_diag, jnp.ones((rows_dev, nkeys), BF16))
    usable = (query_seg == key_seg) | (
        iota((rows_dev, nkeys), 0) == iota((rows_dev, nkeys), 1)
    )
    usable = jnp.where(usable, 1.0, 0.0)
    usable = jnp.concatenate([usable, usable], axis=0) > 0.5
    kept_column = dot(mask_diag, jnp.ones((rows_dev, width), BF16)) > 0.5
    normed = norm_rows(patches).astype(BF16)

    edge_right.wait_recv()
    edge_left.wait_recv()
    own_rows = xwin[EDGE : EDGE + KEPT].astype(F32)
    kept = jnp.concatenate(
        [
            own_rows[:EDGE]
            + lwin[WINDOW - EDGE : WINDOW].astype(F32),
            own_rows[EDGE : KEPT - EDGE],
            own_rows[KEPT - EDGE :] + rwin[0:EDGE].astype(F32),
        ],
        axis=0,
    )
    nkv, nq = 4 * nx * KEPT, nz * KEPT
    normed_kept = norm_rows(kept).astype(BF16)

    def kv_slots(p, first, count):
        return kvbuf.at[p * nkv + first * KEPT : p * nkv + (first + count) * KEPT]

    def q_slot(p, k):
        return qbuf.at[p * nq + k * KEPT : p * nq + (k + 1) * KEPT]

    far_first = sorted(range(1, nz), key=lambda k: -min(k, nz - k))
    far_x = sorted(range(nx), key=lambda k: -min(k, nx - k))
    q_z, kv_x, kv_xy, kv_s = [], [], [], []
    for p in range(npairs):
        q_z.append([])
        kv_x.append([])
        kv_xy.append([])
        for load in pair_loads[3 * p : 3 * (p + 1)]:
            load.wait()
        qkv = dot(normed_kept, wproj[:, 384 * p : 384 * (p + 1)])
        queries = qkv[:, :128].astype(BF16).astype(F32) * 0.125
        qbuf[p * nq : p * nq + KEPT] = queries.astype(BF16)
        kvbuf[p * nkv : p * nkv + KEPT] = qkv[:, 128:].astype(BF16)
        own_kv = kv_slots(p, 0, 1)
        for n in range(max(nx, nz)):
            if n < nx:
                k = far_x[n]
                kv_xy[p].append(send(own_kv, kv_slots(p, nx + (nx - k) % nx, 1), xypeer[k]))
            if n < nz - 1:
                k = far_first[n]
                q_z[p].append(send(q_slot(p, 0), q_slot(p, nz - k), zpeer[k]))
            if n < nx - 1:
                k = far_x[n]
                kv_x[p].append(send(own_kv, kv_slots(p, nx - k, 1), xpeer[k]))
        kv_s.append([send(own_kv, kv_slots(p, 2 * nx, 1), sibling)])

    loads[6].wait()
    cross_query = dot(normed, wproj[:, 3 * half :]).astype(BF16).astype(F32) * 0.125
    cross_query = cross_query.astype(BF16)

    def project_keys(rows, first, last):
        for p in range(npairs):
            columns = wproj[:, 384 * p + 128 : 384 * (p + 1)]
            keys[first:last, 256 * p : 256 * (p + 1)] = dot(rows, columns).astype(BF16)

    project_keys(normed, 0, rows_dev)

    halo_right.wait_recv()
    halo_left.wait_recv()
    near = jnp.concatenate([lwin[...], rwin[...]], axis=0)
    project_keys(norm_rows(near).astype(BF16), rows_dev, nkeys)

    pairs = []

    def cross_pair(i):
        numerator, denominator = attend_pair(
            cross_query[:, 128 * i : 128 * (i + 1)],
            keys[:, 256 * i : 256 * i + 128],
            keys[:, 256 * i + 128 : 256 * (i + 1)],
            usable,
        )
        pairs.append((numerator / denominator).astype(BF16))

    for i in range(npairs):
        cross_pair(i)
    loads[7].wait()
    cross_out[...] = dot(jnp.concatenate(pairs, axis=1), wco[...]).astype(BF16)

    half_mod = lax.rem(iota((1, 128), 1), 64)
    block = npairs * KEPT + 16
    head_lane = 64 * lax.rem(iota((16, 128), 0), 2) + 16 * (iota((16, 128), 0) // 2)
    pick = jnp.where(iota((16, 128), 1) == head_lane, 1.0, 0.0)
    pick = jnp.where(iota((16, 128), 0) < 2 * npairs, pick, 0.0).astype(BF16)
    totals, rs_move, packed = [], [], None
    for p in range(npairs):
        for copy in kv_x[p]:
            copy.wait_recv()
        kv_s[p].append(send(kv_slots(p, 1, nx - 1), kv_slots(p, 2 * nx + 1, nx - 1), sibling))
        for copy in kv_xy[p]:
            copy.wait_recv()
        kv_s[p].append(send(kv_slots(p, nx, nx), kv_slots(p, 3 * nx, nx), sibling))
        if p == 0:
            cross_move = send(cross_out, cross_in, partner)
        for copy in q_z[p]:
            copy.wait_recv()
        ring = qbuf[p * nq : (p + 1) * nq]
        first = slice(p * nkv, p * nkv + nkv // 2)
        second = slice(p * nkv + nkv // 2, (p + 1) * nkv)
        num, den = attend_pair(ring, kvbuf[first, :128], kvbuf[first, 128:], None)
        for copy in kv_s[p]:
            copy.wait_recv()
        num2, den2 = attend_pair(ring, kvbuf[second, :128], kvbuf[second, 128:], None)
        num, den = num + num2, den + den2
        packed = den if p == 0 else jnp.where(half_mod >= 16 * p, den, packed)
        totals.append(num[:KEPT])
        num = num.astype(BF16)
        for k in far_first + [0]:
            rows = slice(k * KEPT, (k + 1) * KEPT)
            there = k * block + p * KEPT
            count = KEPT
            if k:
                rsout[there : there + KEPT] = num[rows]
            if p == npairs - 1:
                own = jnp.concatenate([packed[rows], jnp.zeros((128 - KEPT, 128), F32)], axis=0)
                by_head = dot_t(pick, own.astype(BF16))
                count = KEPT + 16
                if k:
                    rsout[there + KEPT : there + count] = by_head.astype(BF16)
                else:
                    totals.append(by_head)
            if k:
                back = (nz - k) * block + p * KEPT
                rs_move.append(
                    send(rsout.at[there : there + count], rsin.at[back : back + count], zpeer[k])
                )

    for p in range(npairs + 1):
        for copy in rs_move[p * (nz - 1) : (p + 1) * (nz - 1)]:
            copy.wait_recv()
        for k in range(1, nz):
            there = k * block + p * KEPT
            totals[p] += rsin[there : there + totals[p].shape[0]].astype(F32)
    by_head = totals[npairs]
    inverse = jnp.where(by_head > 0.0, 1.0 / by_head, 0.0)
    coarse = inverse.astype(BF16)
    fine = (inverse - coarse.astype(F32)).astype(BF16)
    widen = jnp.where(iota((16, half), 1) // 64 == iota((16, half), 0), 1.0, 0.0).astype(BF16)
    inverse = (dot_0(coarse, widen) + dot_0(fine, widen))[:KEPT]
    attention = [
        (totals[p] * inverse[:, 128 * p : 128 * (p + 1)]).astype(BF16) for p in range(npairs)
    ]
    loads[8].wait()
    attn_out[...] = dot(jnp.concatenate(attention, axis=1), wo[...]).astype(BF16)
    attn_move = send(attn_out, attn_in, partner)
    loads[9].wait()
    loads[10].wait()
    attn_move.wait_recv()
    hidden = kept + (attn_out[...].astype(F32) + attn_in[...].astype(F32))
    edge_hidden[0:EDGE] = hidden[:EDGE]
    edge_hidden[EDGE : 2 * EDGE] = hidden[KEPT - EDGE :]
    hidden_right = send_right(edge_hidden.at[EDGE : 2 * EDGE], left_hidden, right_side)
    hidden_left = send_left(edge_hidden.at[0:EDGE], right_hidden, left_side)
    gated = jax.nn.gelu(dot(norm_rows(hidden).astype(BF16), wu[...]), approximate=True)
    down_out[...] = dot(gated.astype(BF16), wd[...]).astype(BF16)
    ends = []
    for n, side in enumerate((mp, 1 - mp)):
        there = slice(n * EDGE, (n + 1) * EDGE)
        ends.append(send_right(down_out.at[KEPT - EDGE : KEPT], left_down.at[there], (right, side)))
        ends.append(send_left(down_out.at[0:EDGE], right_down.at[there], (left, side)))
    down_move = send(down_out, down_in, partner)
    hidden_right.wait_recv()
    hidden_left.wait_recv()
    down_move.wait_recv()
    own_result = hidden + (down_out[...].astype(F32) + down_in[...].astype(F32))
    for copy in ends:
        copy.wait_recv()

    def edge_result(base_ref, parts_ref):
        parts = parts_ref[...].astype(F32)
        return base_ref[...] + (parts[:EDGE] + parts[EDGE:])

    cross_move.wait_recv()
    pruned = patches.astype(F32) + (cross_out[...].astype(F32) + cross_in[...].astype(F32))

    finished = jnp.concatenate(
        [
            edge_result(left_hidden, left_down),
            own_result,
            edge_result(right_hidden, right_down),
        ],
        axis=0,
    )
    spread = dot_0(own_place, finished.astype(BF16))
    out_ref[...] = jnp.where(kept_column, spread, pruned).astype(BF16)

    for copy in started:
        copy.wait_send()


def body(nx, nz, patches, keep_mask, segment, *weights):
    rows, width = patches.shape
    half = weights[0].shape[1]
    hidden = weights[6].shape[1]
    ntm = nx * nz * 4
    npairs = half // 128
    copies = 14 + npairs * (2 * nx + 2 + 2 * (nz - 1))
    vmem = lambda *shape: pltpu.VMEM(shape, BF16)
    return pl.pallas_call(
        functools.partial(kernel, nx, nz),
        out_shape=pltpu.VMEM((rows, width), BF16),
        in_specs=[pl.BlockSpec(memory_space=pl.ANY)] * 11,
        out_specs=pl.BlockSpec(memory_space=pltpu.VMEM),
        scratch_shapes=[
            vmem(rows, width),
            pltpu.VMEM((ntm * rows // 128, 128), jnp.int32),
            pltpu.VMEM((ntm * rows // 128, 128), jnp.int32),
            vmem(width, 4 * half),
            vmem(half, width),
            vmem(half, width),
            vmem(width, hidden),
            vmem(hidden, width),
            vmem(WINDOW, width),
            vmem(WINDOW, width),
            vmem(WINDOW, width),
            vmem(npairs * 4 * nx * KEPT, 256),
            vmem(npairs * nz * KEPT, 128),
            vmem(nz * (npairs * KEPT + 16), 128),
            vmem(nz * (npairs * KEPT + 16), 128),
            vmem(rows + 2 * WINDOW, 2 * half),
            vmem(KEPT, width),
            vmem(KEPT, width),
            vmem(rows, width),
            vmem(rows, width),
            vmem(KEPT, width),
            vmem(KEPT, width),
            pltpu.VMEM((2 * EDGE, width), F32),
            pltpu.VMEM((EDGE, width), F32),
            pltpu.VMEM((EDGE, width), F32),
            vmem(2 * EDGE, width),
            vmem(2 * EDGE, width),
            pltpu.SemaphoreType.DMA((8 + 3 * npairs,)),
            pltpu.SemaphoreType.DMA((copies,)),
            pltpu.SemaphoreType.DMA((copies,)),
        ],
        compiler_params=pltpu.CompilerParams(
            collective_id=0, has_side_effects=True, vmem_limit_bytes=60 * 1024 * 1024
        ),
    )(patches, keep_mask.reshape(-1, 128), segment.reshape(-1, 128), *weights)


def solution(mesh):
    placed = (
        P("tm", None),
        P(),
        P(),
        P(None, "mp"),
        P(None, "mp"),
        P(None, "mp"),
        P("mp", None),
        P(None, "mp"),
        P("mp", None),
        P(None, "mp"),
        P("mp", None),
    )
    ntm = mesh.shape["tm"]
    nx = 4 if ntm == 128 else 2
    return jax.shard_map(
        functools.partial(body, nx, ntm // (4 * nx)),
        mesh=mesh,
        in_specs=placed,
        out_specs=P("tm", None),
        check_vma=False,
    )
```

```python
import functools

import jax
import jax.numpy as jnp
from jax import lax
from jax.experimental import pallas as pl
from jax.experimental.pallas import tpu as pltpu
from jax.sharding import PartitionSpec as P

KEPT = 48
EDGE = 16
WINDOW = KEPT + 2 * EDGE
F32 = jnp.float32
BF16 = jnp.bfloat16


def norm_rows(values):
    values = values.astype(F32)
    center = values - jnp.mean(values, axis=-1, keepdims=True)
    return center * lax.rsqrt(jnp.mean(center * center, axis=-1, keepdims=True) + 1e-05)


def dot(a, b):
    return jnp.dot(a, b, preferred_element_type=F32)


def dot_t(a, b):
    return lax.dot_general(a, b, (((1,), (1,)), ((), ())), preferred_element_type=F32)


def dot_0(a, b):
    return lax.dot_general(a, b, (((0,), (0,)), ((), ())), preferred_element_type=F32)


def iota(shape, dim):
    return lax.broadcasted_iota(jnp.int32, shape, dim)


def attend_pair(queries, keys, values, usable):
    rows = queries.shape[0]
    low = iota((rows, 128), 1) < 64
    zero = jnp.zeros_like(queries)
    both = jnp.concatenate([jnp.where(low, queries, zero), jnp.where(low, zero, queries)], axis=0)
    weight = jnp.exp(dot_t(both, keys))
    if usable is not None:
        weight = jnp.where(usable, weight, 0.0)
    ones = jnp.ones((keys.shape[0], 128), BF16)
    total = dot(weight.astype(BF16), jnp.concatenate([values, ones], axis=1))
    numerator = jnp.where(low, total[:rows, :128], total[rows:, :128])
    denominator = jnp.where(low, total[:rows, 128:], total[rows:, 128:])
    return numerator, denominator


class Move:
    def __init__(self, copy, going, coming):
        self.copy, self.going, self.coming = copy, going, coming

    def start(self):
        self.run(self.going, self.copy.start)

    def wait_recv(self):
        self.run(self.coming, self.copy.wait_recv)

    def wait_send(self):
        self.run(self.going, self.copy.wait_send)

    def run(self, condition, step):
        if condition is None:
            step()
        else:
            pl.when(condition)(lambda: step())


def kernel(
    nx,
    nz,
    patches_hbm,
    mask_hbm,
    seg_hbm,
    wq_hbm,
    wk_hbm,
    wv_hbm,
    wo_hbm,
    wcq_hbm,
    wco_hbm,
    wu_hbm,
    wd_hbm,
    out_ref,
    patches_ref,
    mask_ref,
    seg_ref,
    wproj,
    wo,
    wco,
    wu,
    wd,
    xwin,
    lwin,
    rwin,
    kvbuf,
    qbuf,
    rsout,
    rsin,
    keys,
    attn_out,
    attn_in,
    cross_out,
    cross_in,
    down_out,
    down_in,
    edge_hidden,
    left_hidden,
    right_hidden,
    left_down,
    right_down,
    wsem,
    ssem,
    rsem,
):
    ntm = nx * nz * 4
    rows_dev, width = patches_hbm.shape
    half = wq_hbm.shape[1]
    me = lax.axis_index("tm")
    mp = lax.axis_index("mp")
    core = lax.rem(me, 2)
    yh = lax.rem(me // 2, 2)
    z = lax.rem(me // 4, nz)
    x = me // (4 * nz)
    sibling = (me + 1 - 2 * core, mp)
    ypart = me + 2 - 4 * yh
    right = lax.rem(me + 1, ntm)
    left = lax.rem(me + ntm - 1, ntm)
    right_side = (right, mp + core * (1 - 2 * mp))
    left_side = (left, mp + (1 - core) * (1 - 2 * mp))
    partner = (me, 1 - mp)
    zpeer = [(me + 4 * (lax.rem(z + k, nz) - z), mp) for k in range(nz)]
    xpeer = [(me + 4 * nz * (lax.rem(x + k, nx) - x), mp) for k in range(nx)]
    xypeer = [(ypart + 4 * nz * (lax.rem(x + k, nx) - x), mp) for k in range(nx)]
    has_left, has_right = me > 0, me < ntm - 1

    barrier = pltpu.get_barrier_semaphore()

    def greet(targets):
        for target in targets:
            pl.semaphore_signal(
                barrier, inc=1, device_id=target, device_id_type=pl.DeviceIdType.MESH
            )

    fixed = [sibling, partner] + zpeer[1:] + xpeer[1:] + xypeer
    greet(fixed)
    pl.when(has_left)(lambda: greet([(left, mp), (left, 1 - mp)]))
    pl.when(has_right)(lambda: greet([(right, mp), (right, 1 - mp)]))
    greeted = len(fixed) + 2 * jnp.minimum(me, 1) + 2 * jnp.minimum(ntm - 1 - me, 1)

    sources = [
        (mask_hbm, mask_ref),
        (patches_hbm, patches_ref),
        (seg_hbm, seg_ref),
        (wq_hbm, wproj.at[:, 0:half]),
        (wk_hbm, wproj.at[:, half : 2 * half]),
        (wv_hbm, wproj.at[:, 2 * half : 3 * half]),
        (wcq_hbm, wproj.at[:, 3 * half : 4 * half]),
        (wco_hbm, wco),
        (wo_hbm, wo),
        (wu_hbm, wu),
        (wd_hbm, wd),
    ]
    loads = []
    for i, (source, target) in enumerate(sources):
        load = pltpu.make_async_copy(source, target, wsem.at[i])
        load.start()
        loads.append(load)

    counter = [0]
    started = []

    def send(source, target, where, going=None, coming=None):
        i = counter[0]
        counter[0] += 1
        copy = pltpu.make_async_remote_copy(
            src_ref=source,
            dst_ref=target,
            send_sem=ssem.at[i],
            recv_sem=rsem.at[i],
            device_id=where,
            device_id_type=pl.DeviceIdType.MESH,
        )
        move = Move(copy, going, coming)
        move.start()
        started.append(move)
        return move

    def send_right(source, target, where):
        return send(source, target, where, has_right, has_left)

    def send_left(source, target, where):
        return send(source, target, where, has_left, has_right)

    loads[0].wait()
    mask = mask_ref[...].astype(F32)
    place = iota(mask.shape, 0) * 128 + iota(mask.shape, 1)
    before = jnp.where(place < me * rows_dev, mask, 0.0)
    base = jnp.sum(jnp.sum(before, axis=1, keepdims=True), axis=0, keepdims=True)
    base = base - (KEPT * me).astype(F32)

    def run_of(ref, index):
        first = index * rows_dev // 128
        both = jnp.concatenate([ref[pl.ds(first, 1), :], ref[pl.ds(first + 1, 1), :]], axis=1)
        phase = lax.rem(index, 4)
        row = both[:, 0:rows_dev]
        for k in range(1, 4):
            row = jnp.where(phase == k, both[:, 32 * k : 32 * k + rows_dev], row)
        return row.astype(F32)

    own_mask = run_of(mask_ref, me)
    left_mask = jnp.where(me > 0, run_of(mask_ref, left), 0.0)
    right_mask = jnp.where(me < ntm - 1, run_of(mask_ref, right), 0.0)
    earlier = (iota((rows_dev, rows_dev), 0) < iota((rows_dev, rows_dev), 1)).astype(F32)
    earlier = earlier.astype(BF16)

    def window(mask_row, base_row):
        rank = dot(jnp.broadcast_to(mask_row, (16, rows_dev)).astype(BF16), earlier)[0:1]
        slot = jnp.where(mask_row > 0.5, rank + base_row + float(EDGE), -1.0)
        grid = iota((WINDOW, rows_dev), 0).astype(F32)
        return jnp.where(grid == slot, 1.0, 0.0).astype(BF16)

    own_place = window(own_mask, base)
    loads[1].wait()
    patches = patches_ref[...]
    xwin[...] = dot(own_place, patches).astype(BF16)

    def clear(*refs):
        for ref in refs:
            ref[...] = jnp.zeros(ref.shape, ref.dtype)

    pl.when(me == 0)(lambda: clear(lwin, left_hidden, left_down))
    pl.when(me == ntm - 1)(lambda: clear(rwin, right_hidden, right_down))

    pl.semaphore_wait(barrier, greeted)

    edge_right = send_right(xwin.at[KEPT + EDGE : WINDOW], lwin.at[KEPT + EDGE : WINDOW], right_side)
    edge_left = send_left(xwin.at[0:EDGE], rwin.at[0:EDGE], left_side)
    halo_right = send_right(xwin.at[0 : KEPT + EDGE], lwin.at[0 : KEPT + EDGE], right_side)
    halo_left = send_left(xwin.at[EDGE:WINDOW], rwin.at[EDGE:WINDOW], left_side)

    loads[2].wait()
    own_seg = run_of(seg_ref, me) + 1.0
    left_seg = run_of(seg_ref, left) + 1.0
    right_seg = run_of(seg_ref, right) + 1.0
    own_count = jnp.sum(own_mask, axis=1, keepdims=True)
    left_count = jnp.sum(left_mask, axis=1, keepdims=True)
    left_place = window(left_mask, base - left_count + float(KEPT))
    right_place = window(right_mask, base + own_count - float(KEPT))

    def key_segments(mask_place, seg_row):
        return dot_t(jnp.broadcast_to(seg_row, (16, rows_dev)).astype(BF16), mask_place)[0:1]

    key_seg = jnp.concatenate(
        [
            jnp.where(own_mask > 0.5, own_seg, 0.0),
            key_segments(left_place, left_seg),
            key_segments(right_place, right_seg),
        ],
        axis=1,
    )
    nkeys = rows_dev + 2 * WINDOW
    same = iota((rows_dev, rows_dev), 0) == iota((rows_dev, rows_dev), 1)
    seg_diag = jnp.where(same, own_seg, 0.0).astype(BF16)
    mask_diag = jnp.where(same, own_mask, 0.0).astype(BF16)
    query_seg = dot(seg_diag, jnp.ones((rows_dev, nkeys), BF16))
    usable = (query_seg == key_seg) | (
        iota((rows_dev, nkeys), 0) == iota((rows_dev, nkeys), 1)
    )
    usable = jnp.where(usable, 1.0, 0.0)
    usable = jnp.concatenate([usable, usable], axis=0) > 0.5
    kept_column = dot(mask_diag, jnp.ones((rows_dev, width), BF16)) > 0.5
    normed = norm_rows(patches).astype(BF16)

    edge_right.wait_recv()
    edge_left.wait_recv()
    own_rows = xwin[EDGE : EDGE + KEPT].astype(F32)
    kept = jnp.concatenate(
        [
            own_rows[:EDGE]
            + lwin[WINDOW - EDGE : WINDOW].astype(F32),
            own_rows[EDGE : KEPT - EDGE],
            own_rows[KEPT - EDGE :] + rwin[0:EDGE].astype(F32),
        ],
        axis=0,
    )
    for load in loads[3:6]:
        load.wait()
    qkv = dot(norm_rows(kept).astype(BF16), wproj[:, : 3 * half])
    queries = (qkv[:, :half].astype(BF16).astype(F32) * 0.125).astype(BF16)
    kept_kv = qkv[:, half:].astype(BF16)
    npairs = half // 128
    nkv, nq = 4 * nx * KEPT, nz * KEPT
    for p in range(npairs):
        lanes = slice(128 * p, 128 * (p + 1))
        qbuf[p * nq : p * nq + KEPT] = queries[:, lanes]
        kvbuf[p * nkv : p * nkv + KEPT, :128] = kept_kv[:, :half][:, lanes]
        kvbuf[p * nkv : p * nkv + KEPT, 128:] = kept_kv[:, half:][:, lanes]

    def kv_slots(p, first, count):
        return kvbuf.at[p * nkv + first * KEPT : p * nkv + (first + count) * KEPT]

    def q_slot(p, k):
        return qbuf.at[p * nq + k * KEPT : p * nq + (k + 1) * KEPT]

    far_first = sorted(range(1, nz), key=lambda k: -min(k, nz - k))
    far_x = sorted(range(nx), key=lambda k: -min(k, nx - k))
    q_z, kv_x, kv_xy, kv_s = [], [], [], []
    for p in range(npairs):
        q_z.append([])
        kv_x.append([])
        kv_xy.append([])
        own_kv = kv_slots(p, 0, 1)
        for n in range(max(nx, nz)):
            if n < nx:
                k = far_x[n]
                kv_xy[p].append(send(own_kv, kv_slots(p, nx + (nx - k) % nx, 1), xypeer[k]))
            if n < nz - 1:
                k = far_first[n]
                q_z[p].append(send(q_slot(p, 0), q_slot(p, nz - k), zpeer[k]))
            if n < nx - 1:
                k = far_x[n]
                kv_x[p].append(send(own_kv, kv_slots(p, nx - k, 1), xpeer[k]))
        kv_s.append([send(own_kv, kv_slots(p, 2 * nx, 1), sibling)])

    loads[6].wait()
    own_proj = dot(normed, wproj[:, half:])
    keys[0:rows_dev] = own_proj[:, : 2 * half].astype(BF16)
    cross_query = (own_proj[:, 2 * half :].astype(BF16).astype(F32) * 0.125).astype(BF16)

    halo_right.wait_recv()
    halo_left.wait_recv()
    near = jnp.concatenate([lwin[...], rwin[...]], axis=0)
    keys[rows_dev:nkeys] = dot(
        norm_rows(near).astype(BF16), wproj[:, half : 3 * half]
    ).astype(BF16)

    pairs = []

    def cross_pair(i):
        numerator, denominator = attend_pair(
            cross_query[:, 128 * i : 128 * (i + 1)],
            keys[:, 128 * i : 128 * (i + 1)],
            keys[:, half + 128 * i : half + 128 * (i + 1)],
            usable,
        )
        pairs.append((numerator / denominator).astype(BF16))

    for i in range(npairs):
        cross_pair(i)
    loads[7].wait()
    cross_out[...] = dot(jnp.concatenate(pairs, axis=1), wco[...]).astype(BF16)

    half_mod = lax.rem(iota((1, 128), 1), 64)
    block = npairs * KEPT + 16
    head_lane = 64 * lax.rem(iota((16, 128), 0), 2) + 16 * (iota((16, 128), 0) // 2)
    pick = jnp.where(iota((16, 128), 1) == head_lane, 1.0, 0.0)
    pick = jnp.where(iota((16, 128), 0) < 2 * npairs, pick, 0.0).astype(BF16)
    totals, rs_move, packed = [], [], None
    for p in range(npairs):
        for copy in kv_x[p]:
            copy.wait_recv()
        kv_s[p].append(send(kv_slots(p, 1, nx - 1), kv_slots(p, 2 * nx + 1, nx - 1), sibling))
        for copy in kv_xy[p]:
            copy.wait_recv()
        kv_s[p].append(send(kv_slots(p, nx, nx), kv_slots(p, 3 * nx, nx), sibling))
        if p == 0:
            cross_move = send(cross_out, cross_in, partner)
        for copy in q_z[p]:
            copy.wait_recv()
        ring = qbuf[p * nq : (p + 1) * nq]
        first = slice(p * nkv, p * nkv + nkv // 2)
        second = slice(p * nkv + nkv // 2, (p + 1) * nkv)
        num, den = attend_pair(ring, kvbuf[first, :128], kvbuf[first, 128:], None)
        for copy in kv_s[p]:
            copy.wait_recv()
        num2, den2 = attend_pair(ring, kvbuf[second, :128], kvbuf[second, 128:], None)
        num, den = num + num2, den + den2
        packed = den if p == 0 else jnp.where(half_mod >= 16 * p, den, packed)
        totals.append(num[:KEPT])
        num = num.astype(BF16)
        for k in far_first + [0]:
            rows = slice(k * KEPT, (k + 1) * KEPT)
            there = k * block + p * KEPT
            count = KEPT
            if k:
                rsout[there : there + KEPT] = num[rows]
            if p == npairs - 1:
                own = jnp.concatenate([packed[rows], jnp.zeros((128 - KEPT, 128), F32)], axis=0)
                by_head = dot_t(pick, own.astype(BF16))
                count = KEPT + 16
                if k:
                    rsout[there + KEPT : there + count] = by_head.astype(BF16)
                else:
                    totals.append(by_head)
            if k:
                back = (nz - k) * block + p * KEPT
                rs_move.append(
                    send(rsout.at[there : there + count], rsin.at[back : back + count], zpeer[k])
                )

    for p in range(npairs + 1):
        for copy in rs_move[p * (nz - 1) : (p + 1) * (nz - 1)]:
            copy.wait_recv()
        for k in range(1, nz):
            there = k * block + p * KEPT
            totals[p] += rsin[there : there + totals[p].shape[0]].astype(F32)
    by_head = totals[npairs]
    inverse = jnp.where(by_head > 0.0, 1.0 / by_head, 0.0)
    coarse = inverse.astype(BF16)
    fine = (inverse - coarse.astype(F32)).astype(BF16)
    widen = jnp.where(iota((16, half), 1) // 64 == iota((16, half), 0), 1.0, 0.0).astype(BF16)
    inverse = (dot_0(coarse, widen) + dot_0(fine, widen))[:KEPT]
    attention = [
        (totals[p] * inverse[:, 128 * p : 128 * (p + 1)]).astype(BF16) for p in range(npairs)
    ]
    loads[8].wait()
    attn_out[...] = dot(jnp.concatenate(attention, axis=1), wo[...]).astype(BF16)
    attn_move = send(attn_out, attn_in, partner)
    loads[9].wait()
    loads[10].wait()
    attn_move.wait_recv()
    hidden = kept + (attn_out[...].astype(F32) + attn_in[...].astype(F32))
    edge_hidden[0:EDGE] = hidden[:EDGE]
    edge_hidden[EDGE : 2 * EDGE] = hidden[KEPT - EDGE :]
    hidden_right = send_right(edge_hidden.at[EDGE : 2 * EDGE], left_hidden, right_side)
    hidden_left = send_left(edge_hidden.at[0:EDGE], right_hidden, left_side)
    gated = jax.nn.gelu(dot(norm_rows(hidden).astype(BF16), wu[...]), approximate=True)
    down_out[...] = dot(gated.astype(BF16), wd[...]).astype(BF16)
    down_move = send(down_out, down_in, partner)
    ends = []
    for n, side in enumerate((mp, 1 - mp)):
        there = slice(n * EDGE, (n + 1) * EDGE)
        ends.append(send_right(down_out.at[KEPT - EDGE : KEPT], left_down.at[there], (right, side)))
        ends.append(send_left(down_out.at[0:EDGE], right_down.at[there], (left, side)))
    hidden_right.wait_recv()
    hidden_left.wait_recv()
    down_move.wait_recv()
    own_result = hidden + (down_out[...].astype(F32) + down_in[...].astype(F32))
    for copy in ends:
        copy.wait_recv()

    def edge_result(base_ref, parts_ref):
        parts = parts_ref[...].astype(F32)
        return base_ref[...] + (parts[:EDGE] + parts[EDGE:])

    cross_move.wait_recv()
    pruned = patches.astype(F32) + (cross_out[...].astype(F32) + cross_in[...].astype(F32))

    finished = jnp.concatenate(
        [
            edge_result(left_hidden, left_down),
            own_result,
            edge_result(right_hidden, right_down),
        ],
        axis=0,
    )
    spread = dot_0(own_place, finished.astype(BF16))
    out_ref[...] = jnp.where(kept_column, spread, pruned).astype(BF16)

    for copy in started:
        copy.wait_send()


def body(nx, nz, patches, keep_mask, segment, *weights):
    rows, width = patches.shape
    half = weights[0].shape[1]
    hidden = weights[6].shape[1]
    ntm = nx * nz * 4
    npairs = half // 128
    copies = 14 + npairs * (2 * nx + 2 + 2 * (nz - 1))
    vmem = lambda *shape: pltpu.VMEM(shape, BF16)
    return pl.pallas_call(
        functools.partial(kernel, nx, nz),
        out_shape=pltpu.VMEM((rows, width), BF16),
        in_specs=[pl.BlockSpec(memory_space=pl.ANY)] * 11,
        out_specs=pl.BlockSpec(memory_space=pltpu.VMEM),
        scratch_shapes=[
            vmem(rows, width),
            pltpu.VMEM((ntm * rows // 128, 128), jnp.int32),
            pltpu.VMEM((ntm * rows // 128, 128), jnp.int32),
            vmem(width, 4 * half),
            vmem(half, width),
            vmem(half, width),
            vmem(width, hidden),
            vmem(hidden, width),
            vmem(WINDOW, width),
            vmem(WINDOW, width),
            vmem(WINDOW, width),
            vmem(npairs * 4 * nx * KEPT, 256),
            vmem(npairs * nz * KEPT, 128),
            vmem(nz * (npairs * KEPT + 16), 128),
            vmem(nz * (npairs * KEPT + 16), 128),
            vmem(rows + 2 * WINDOW, 2 * half),
            vmem(KEPT, width),
            vmem(KEPT, width),
            vmem(rows, width),
            vmem(rows, width),
            vmem(KEPT, width),
            vmem(KEPT, width),
            pltpu.VMEM((2 * EDGE, width), F32),
            pltpu.VMEM((EDGE, width), F32),
            pltpu.VMEM((EDGE, width), F32),
            vmem(2 * EDGE, width),
            vmem(2 * EDGE, width),
            pltpu.SemaphoreType.DMA((11,)),
            pltpu.SemaphoreType.DMA((copies,)),
            pltpu.SemaphoreType.DMA((copies,)),
        ],
        compiler_params=pltpu.CompilerParams(
            collective_id=0, has_side_effects=True, vmem_limit_bytes=60 * 1024 * 1024
        ),
    )(patches, keep_mask.reshape(-1, 128), segment.reshape(-1, 128), *weights)


def solution(mesh):
    placed = (
        P("tm", None),
        P(),
        P(),
        P(None, "mp"),
        P(None, "mp"),
        P(None, "mp"),
        P("mp", None),
        P(None, "mp"),
        P("mp", None),
        P(None, "mp"),
        P("mp", None),
    )
    ntm = mesh.shape["tm"]
    nx = 4 if ntm == 128 else 2
    return jax.shard_map(
        functools.partial(body, nx, ntm // (4 * nx)),
        mesh=mesh,
        in_specs=placed,
        out_specs=P("tm", None),
        check_vma=False,
    )
```
